512 devices in a mesh: pipe: 4 (over z_hi, core), seq: 32 (over y, x), dp: 4 (over z_lo).
Axes of the slice: x: 4, y: 8, z: 8 (z_hi: 2, z_lo: 4; z = z_hi * 4 + z_lo), core: 2. Of those that a mesh axis runs over, the one named last changes fastest.
Arguments:
- inputs: bfloat16 [4, 2, 2048, 4096], P('dp', None, 'seq'), may hold values from -40 to 40
- weights: bfloat16 [4, 32, 4, 128, 128], P(None, 'seq'), may hold values from -1 to 1, as said below
- gains: float32 [4, 4096], replicated, may hold values from 0.25 to 1.75
- doc_lengths: int32 [4, 2, 48], P('dp'), may hold values from 1 to 64, 2048 in all within a row
Outputs:
- weight_grads: float32 [4, 32, 4, 128, 128], P('pipe', 'seq')
The draws below stay inside these ranges and needn't reach their ends.
Inputs may be any that keep to these rules, and one draw needn't show every extreme that they name: In each block weights[s, j, m] every entry is 0 or plus or minus one positive value of that block. `doc_lengths`: the lengths in each row sum to 2048 and are the documents of that micro-batch in order.
All inputs are finite; a program needn't handle non-finite values.
Results may differ from the reference program's by a relative error of at most 0.015.
Values may be sent and summed in bfloat16 or wider, within the bound.
A program may use at most 128 MiB of HBM per device.

```python
import math
import jax
import jax.numpy as jnp
import numpy as np
from jax import lax

HEADS = 32
HEAD_DIM = 128
D = 4096
TOKENS = 2048
MOST = 64
NDOCS = 48
SECTIONS = 4
REPLICAS = 4


def draw_inputs(key, part):
    key = jax.random.fold_in(key, 11)
    base_key = jax.random.fold_in(key, 0)
    row_key = jax.random.fold_in(key, 1)
    column_key = jax.random.fold_in(key, 3)
    shape = (REPLICAS, 2, TOKENS, D)
    columns = 10.0 ** jax.random.uniform(column_key, (1, 1, 1, D), jnp.float32)
    row_scale = 10.0 ** jax.random.uniform(row_key, (REPLICAS, 2, TOKENS, 1), jnp.float32)
    noise = jnp.clip(jax.random.normal(base_key, shape, jnp.float32), -4.0, 4.0)
    return (0.1 * noise * row_scale * columns).astype(jnp.bfloat16)


def draw_weights(key, part):
    key = jax.random.fold_in(key, 23)
    level_key, scale_key = jax.random.split(key)
    levels = jax.random.randint(level_key, (SECTIONS, HEADS, 4, HEAD_DIM, HEAD_DIM), -1, 2).astype(jnp.float32)
    block_scale = jnp.exp(jax.random.uniform(scale_key, (SECTIONS, HEADS, 4, 1, 1), jnp.float32, jnp.log(0.7), jnp.log(2.0)))
    return (levels * block_scale / jnp.sqrt(jnp.float32(HEAD_DIM))).astype(jnp.bfloat16)


def profile(number_of, total, most, slope):
    loads = [(1 << 20) // math.isqrt(rank ** slope) + 1 for rank in range(2, number_of + 1)]
    spare, given = total - most - (number_of - 1), [1] * (number_of - 1)
    while spare > 0:
        candidates = [i for i in range(number_of - 1) if given[i] < most]
        whole, budget = sum([loads[i] for i in candidates]), spare
        for i in candidates:
            addition = min(most - given[i], max(1, budget * loads[i] // whole), spare)
            given[i] = given[i] + addition
            spare = spare - addition
    return np.array([most] + given)


def uneven(key, amount, total, most, skew):
    if amount == 2:
        one = jax.random.randint(key, (), max(1, total - most), min(most, total - 1) + 1)
        return jnp.stack([one, total - one])
    tallies = jnp.asarray(profile(amount, total, most, skew), jnp.int32)
    pairs = (amount - 1) // 2
    source_of, receiver = tallies[1:1 + 2 * pairs:2], tallies[2:2 + 2 * pairs:2]
    margin = jnp.minimum(source_of - 1, most - receiver)
    shifted = jax.random.randint(jax.random.fold_in(key, 1), (pairs,), 0, 1 << 20) % (margin + 1)
    tallies = tallies.at[1:1 + 2 * pairs:2].set(source_of - shifted).at[2:2 + 2 * pairs:2].set(receiver + shifted)
    return tallies[jax.random.permutation(jax.random.fold_in(key, 2), amount)]


def setup_inputs(seed: int = 0) -> dict:
    seeds = jax.random.split(jax.random.key(seed), 5)
    inputs = draw_inputs(jax.random.fold_in(seeds[4], 71), 0)
    weights = draw_weights(jax.random.fold_in(seeds[4], 71), 0)
    gains = jnp.clip(1.0 + 0.15 * jax.random.normal(seeds[2], (SECTIONS, D), jnp.float32), 0.25, 1.75)
    doc_lengths = jax.vmap(lambda own: uneven(own, NDOCS, TOKENS, MOST, 1))(jax.random.split(seeds[3], REPLICAS * 2)).reshape((REPLICAS, 2, NDOCS)).astype(jnp.int32)
    return {"inputs": inputs, "weights": weights, "gains": gains, "doc_lengths": doc_lengths}


EPSILON = 1e-06

def mix(form, left, right):
    return jnp.einsum(form, left.astype(jnp.float32), right.astype(jnp.float32))

def windowed(values, blocks, span):
    shaped = values.reshape((blocks, span) + values.shape[1:])
    earlier = jnp.concatenate([jnp.zeros_like(shaped[:1]), shaped[:-1]], axis=0)
    return jnp.concatenate([earlier, shaped], axis=1)

def unwindow(values, span):
    blocks = values.shape[0]
    inside = values[:, span:]
    later = jnp.concatenate([values[1:, :span], jnp.zeros_like(values[:1, :span])], axis=0)
    return (inside + later).reshape((blocks * span,) + values.shape[2:])

def doc_mask(lengths, total, span):
    ends = jnp.cumsum(lengths).astype(jnp.int32)
    places = jnp.arange(total, dtype=jnp.int32)
    owner = lax.optimization_barrier(jnp.sum((ends[None, :] <= places[:, None]).astype(jnp.int32), axis=1)).astype(jnp.int32)
    blocks = total // span
    owner_q = owner.reshape(blocks, span)
    owner_prev = jnp.concatenate([jnp.full((1, span), -1, jnp.int32), owner_q[:-1]], axis=0)
    owner_k = jnp.concatenate([owner_prev, owner_q], axis=1)
    row_place = jnp.arange(span, dtype=jnp.int32)[:, None]
    col_place = jnp.arange(2 * span, dtype=jnp.int32)[None, :]
    return (owner_q[:, :, None] == owner_k[:, None, :]) & (col_place <= row_place + span)[None]

def head_core(inputs_h, weights_h, allowed, span):
    tokens, heads, width = inputs_h.shape
    blocks = tokens // span
    query = mix('shc,hcd->shd', inputs_h, weights_h[:, 0])
    keys = mix('shc,hcd->shd', inputs_h, weights_h[:, 1])
    values = mix('shc,hcd->shd', inputs_h, weights_h[:, 2]).astype(jnp.bfloat16)
    query_scale = lax.rsqrt(lax.optimization_barrier(jnp.mean(query * query, axis=-1, keepdims=True)) + EPSILON)
    key_scale = lax.rsqrt(lax.optimization_barrier(jnp.mean(keys * keys, axis=-1, keepdims=True)) + EPSILON)
    query_blocks = (query * query_scale).astype(jnp.bfloat16).reshape(blocks, span, heads, width)
    key_window = windowed((keys * key_scale).astype(jnp.bfloat16), blocks, span)
    value_window = windowed(values, blocks, span)
    scores = mix('bqhd,bkhd->bhqk', query_blocks, key_window) * width ** (-0.5)
    raised = jnp.where(allowed[:, None], jnp.exp(scores), 0.0)
    attention = (raised / lax.optimization_barrier(jnp.sum(raised, axis=-1, keepdims=True))).astype(jnp.bfloat16)
    mixed = mix('bhqk,bkhd->bqhd', attention, value_window).astype(jnp.bfloat16).reshape(tokens, heads, width)
    return (query, keys, query_scale, key_scale, query_blocks, key_window, value_window, attention, mixed)

def head_back(inputs_h, weights_h, cached, branch_grad, span):
    query, keys, query_scale, key_scale, query_blocks, key_window, value_window, attention, mixed = cached
    tokens, heads, width = inputs_h.shape
    blocks = tokens // span
    grad_out = mix('shd,she->hde', mixed, branch_grad)
    grad_mixed = mix('she,hde->shd', branch_grad, weights_h[:, 3]).astype(jnp.bfloat16).reshape(blocks, span, heads, width)
    grad_attention = mix('bqhd,bkhd->bhqk', grad_mixed, value_window)
    grad_values = unwindow(mix('bhqk,bqhd->bkhd', attention, grad_mixed), span).astype(jnp.bfloat16)
    chances = attention.astype(jnp.float32)
    grad_scores = (chances * (grad_attention - lax.optimization_barrier(jnp.sum(grad_attention * chances, axis=-1, keepdims=True))) * width ** (-0.5)).astype(jnp.bfloat16)
    unit_query_grad = mix('bhqk,bkhd->bqhd', grad_scores, key_window).reshape(tokens, heads, width)
    unit_key_grad = unwindow(mix('bhqk,bqhd->bkhd', grad_scores, query_blocks), span)
    grad_query = (query_scale * unit_query_grad - query * query_scale ** 3 * lax.optimization_barrier(jnp.mean(unit_query_grad * query, axis=-1, keepdims=True))).astype(jnp.bfloat16)
    grad_keys = (key_scale * unit_key_grad - keys * key_scale ** 3 * lax.optimization_barrier(jnp.mean(unit_key_grad * keys, axis=-1, keepdims=True))).astype(jnp.bfloat16)
    grad_in = mix('shd,hcd->shc', grad_query, weights_h[:, 0]) + mix('shd,hcd->shc', grad_keys, weights_h[:, 1]) + mix('shd,hcd->shc', grad_values, weights_h[:, 2])
    grads = jnp.stack([mix('shc,shd->hcd', inputs_h, grad_query), mix('shc,shd->hcd', inputs_h, grad_keys), mix('shc,shd->hcd', inputs_h, grad_values), grad_out], axis=1)
    return (grad_in.astype(jnp.bfloat16), grads)

def section_forward(state, gain_row, weights_h, allowed):
    wide = state.astype(jnp.float32)
    scale = lax.rsqrt(lax.optimization_barrier(jnp.mean(wide * wide, axis=-1, keepdims=True)) + EPSILON)
    normed = (wide * scale * gain_row).astype(jnp.bfloat16)
    shaped = normed.reshape(normed.shape[0], HEADS, HEAD_DIM)
    cached = head_core(shaped, weights_h, allowed, MOST)
    branch = mix('shd,hde->she', cached[-1], weights_h[:, 3]).astype(jnp.bfloat16).reshape(normed.shape)
    return ((wide + branch.astype(jnp.float32)).astype(jnp.bfloat16), shaped, scale)

def section_backward(state, shaped, scale, cotangent, gain_row, weights_h, allowed):
    cached = head_core(shaped, weights_h, allowed, MOST)
    grad_h, grads = head_back(shaped, weights_h, cached, cotangent.reshape(shaped.shape), MOST)
    wide = state.astype(jnp.float32)
    pulled = grad_h.reshape(state.shape).astype(jnp.float32) * gain_row
    along = lax.optimization_barrier(jnp.mean(pulled * wide, axis=-1, keepdims=True))
    carried = scale * pulled - wide * scale ** 3 * along
    return ((cotangent.astype(jnp.float32) + carried).astype(jnp.bfloat16), grads)

def reference(inputs, weights, gains, doc_lengths):
    grads = jnp.zeros((SECTIONS, HEADS, 4, HEAD_DIM, HEAD_DIM), jnp.float32)
    for replica in range(REPLICAS):
        for micro in range(2):
            allowed = doc_mask(doc_lengths[replica, micro], TOKENS, MOST)
            state = inputs[replica, micro]
            kept = []
            for section in range(SECTIONS):
                new_state, shaped, scale = section_forward(state, gains[section], weights[section], allowed)
                kept.append((state, shaped, scale))
                state = new_state
            cotangent = state
            for section in range(SECTIONS - 1, -1, -1):
                saved_state, shaped, scale = kept[section]
                cotangent, part_grads = section_backward(saved_state, shaped, scale, cotangent, gains[section], weights[section], allowed)
                grads = grads.at[section].add(part_grads)
    return grads
```

```python
import functools

import jax
import jax.numpy as jnp
from jax import lax
from jax.experimental import pallas as pl
from jax.experimental.pallas import tpu as pltpu
from jax.sharding import PartitionSpec as P

EPSILON = 1e-06
SECTIONS = 4
SPAN = 64
HEAD = 128
GROUP = 128
F32 = jnp.float32
BF16 = jnp.bfloat16
LOG2E = 1.4426950408889634


def dot(a, b):
    return lax.dot_general(a, b, (((1,), (0,)), ((), ())), preferred_element_type=F32)


def dot_nt(a, b):
    return lax.dot_general(a, b, (((1,), (1,)), ((), ())), preferred_element_type=F32)


def dot_tn(a, b):
    return lax.dot_general(a, b, (((0,), (0,)), ((), ())), preferred_element_type=F32)


def kernel(
    cfg,
    inputs_ref,
    weights_ref,
    gains_ref,
    docs_ref,
    grads_ref,
    states,
    normed,
    queries,
    keys,
    values,
    mixed,
    chances,
    scale_q,
    scale_k,
    scale_x,
    mask,
    valid,
    cot,
    grad_mixed,
    grad_normed,
    grad_q,
    grad_k,
    grad_v,
    carry,
    sums,
    gain_rows,
    send1,
    recv1,
    send2,
    recv2,
    in_send,
    in_recv,
    send1_sem,
    recv1_sem,
    send2_sem,
    recv2_sem,
):
    total, seq, width, across = cfg["total"], cfg["seq"], cfg["width"], cfg["across"]
    rows, chunk, chunks = cfg["rows"], cfg["chunk"], cfg["chunks"]
    down = seq // across
    groups, blocks = chunk // GROUP, chunk // SPAN
    all_blocks = rows // SPAN
    place, me = lax.axis_index("pipe"), lax.axis_index("seq")
    micro, half = place // 2, place % 2
    first_block = half * (seq - all_blocks)
    window = first_block * SPAN
    my_x, my_y = me % across, me // across

    barrier = pltpu.get_barrier_semaphore()

    def greet(o, _):
        pl.semaphore_signal(barrier, inc=1, device_id={"seq": (me + o) % seq})
        return 0

    lax.fori_loop(1, seq, greet, 0)
    pl.semaphore_wait(barrier, seq - 1)

    slot = me - first_block
    in_window = (slot >= 0) & (slot < all_blocks)

    def piece(head):
        return inputs_ref.at[0, micro, :, pl.ds(pl.multiple_of(head * HEAD, HEAD), HEAD)]

    @pl.when(in_window)
    def _():
        landing = states.at[0, pl.ds(pl.multiple_of(slot * SPAN, SPAN), SPAN)]

        def send(o, _):
            peer = (me + o) % seq
            pltpu.make_async_remote_copy(
                src_ref=piece(peer),
                dst_ref=landing,
                send_sem=in_send,
                recv_sem=in_recv,
                device_id={"seq": peer},
            ).start()
            return 0

        lax.fori_loop(1, seq, send, 0)
        pltpu.make_async_copy(piece(me), landing, in_recv).start()

    ones = jnp.full((HEAD, HEAD), 1.0 / HEAD, BF16)
    row8 = lax.broadcasted_iota(jnp.int32, (8, HEAD), 0)

    both = docs_ref[0].astype(F32)
    lengths = jnp.where(micro == 0, both[0:1], both[1:2]).astype(BF16)
    count = lengths.shape[1]
    earlier = lax.broadcasted_iota(jnp.int32, (count, HEAD), 0) < lax.broadcasted_iota(
        jnp.int32, (count, HEAD), 1
    )
    starts = dot(jnp.broadcast_to(lengths, (8, count)), jnp.where(earlier, 1.0, 0.0).astype(BF16))[:1]
    mid = total // 2

    def make_mask(b, _):
        base = window + b * SPAN
        token = base + lax.broadcasted_iota(jnp.int32, (SPAN, HEAD), 0)
        key = base - SPAN + lax.broadcasted_iota(jnp.int32, (SPAN, HEAD), 1)
        reach = jnp.where(starts <= token.astype(F32), starts, 0.0)
        begin = jnp.max(reach, axis=1, keepdims=True)
        allowed = (key.astype(F32) >= begin) & (key <= token)
        mask[b] = jnp.where(allowed, 1.0, 0.0)
        late = jnp.where(begin >= mid, 1.0, 0.0)
        mine = jnp.where(half == 1, late, 1.0 - late)
        valid[pl.ds(pl.multiple_of(b * SPAN, SPAN), SPAN)] = jnp.broadcast_to(mine, (SPAN, HEAD)).astype(BF16)
        return 0

    lax.fori_loop(0, all_blocks, make_mask, 0)
    for s in range(SECTIONS):
        keys[s, :SPAN] = jnp.zeros((SPAN, HEAD), BF16)
        values[s, :SPAN] = jnp.zeros((SPAN, HEAD), BF16)
        gain = gains_ref[s : s + 1, pl.ds(pl.multiple_of(me * HEAD, HEAD), HEAD)]
        gain_rows[s] = jnp.broadcast_to(gain, (8, HEAD))
    sums[...] = jnp.zeros_like(sums)

    def packed(terms):
        total_rows = None
        for g, term in enumerate(terms):
            pick = jnp.where(row8 == g, 1.0, 0.0).astype(BF16)
            part = dot_nt(pick, term.astype(BF16))
            total_rows = part if total_rows is None else total_rows + part
        return total_rows

    def spread(row):
        return jnp.transpose(jnp.broadcast_to(row, (HEAD, GROUP)))

    def start1(item, part):
        send1[item] = part
        for o in range(1, across):
            pltpu.make_async_remote_copy(
                src_ref=send1.at[item],
                dst_ref=recv1.at[item, o - 1],
                send_sem=send1_sem.at[item],
                recv_sem=recv1_sem.at[item],
                device_id={"seq": my_y * across + (my_x + o) % across},
            ).start()

    def start2(item):
        pltpu.make_async_copy(recv1.at[item], recv1.at[item], recv1_sem.at[item]).wait()
        part = send1[item]
        for o in range(across - 1):
            part = part + recv1[item, o]
        send2[item] = part
        for o in range(1, down):
            pltpu.make_async_remote_copy(
                src_ref=send2.at[item],
                dst_ref=recv2.at[item, o - 1],
                send_sem=send2_sem.at[item],
                recv_sem=recv2_sem.at[item],
                device_id={"seq": ((my_y + o) % down) * across + my_x},
            ).start()

    def finish(item):
        pltpu.make_async_copy(recv2.at[item], recv2.at[item], recv2_sem.at[item]).wait()
        part = send2[item]
        for o in range(down - 1):
            part = part + recv2[item, o]
        return part

    def span_of(start, size):
        return pl.ds(pl.multiple_of(start, SPAN), size)

    def gain_of(s):
        return gain_rows[s][:1]

    pltpu.make_async_copy(states.at[0], states.at[0], in_recv).wait()

    def begin(c, _):
        terms = []
        for g in range(groups):
            x = states[0, span_of(c * chunk + g * GROUP, GROUP)].astype(F32)
            terms.append(x * x)
        start1(c, packed(terms))
        return 0

    lax.fori_loop(0, chunks, begin, 0)
    lax.fori_loop(0, chunks, lambda c, _: (start2(c), 0)[1], 0)

    def forward(i, _):
        s, c = i // chunks, i % chunks
        base = c * chunk
        rs = lax.rsqrt(finish(i) * (1.0 / width) + EPSILON)
        gain = gain_of(s)
        for g in range(groups):
            at = span_of(base + g * GROUP, GROUP)
            padded = span_of(base + g * GROUP + SPAN, GROUP)
            wide = spread(rs[g : g + 1])
            scale_x[s, at] = wide
            xn = (states[s, at].astype(F32) * wide * gain).astype(BF16)
            normed[s, at] = xn
            q = dot(xn, weights_ref[s, 0, 0])
            k = dot(xn, weights_ref[s, 0, 1])
            values[s, padded] = dot(xn, weights_ref[s, 0, 2]).astype(BF16)
            rq = lax.rsqrt(dot((q * q).astype(BF16), ones) + EPSILON)
            rk = lax.rsqrt(dot((k * k).astype(BF16), ones) + EPSILON)
            scale_q[s, at] = rq
            scale_k[s, at] = rk
            queries[s, at] = (q * rq).astype(BF16)
            keys[s, padded] = (k * rk).astype(BF16)
        for b in range(blocks):
            at = span_of(base + b * SPAN, SPAN)
            near = span_of(base + b * SPAN, 2 * SPAN)
            scores = dot_nt(queries[s, at], keys[s, near])
            raised = jnp.exp2(scores * (LOG2E * HEAD**-0.5)) * mask[c * blocks + b]
            share = (raised / jnp.sum(raised, axis=1, keepdims=True)).astype(BF16)
            chances[s, c * blocks + b] = share
            mixed[s, at] = dot(share, values[s, near]).astype(BF16)
        terms = []
        for g in range(groups):
            at = span_of(base + g * GROUP, GROUP)
            branch = dot(mixed[s, at], weights_ref[s, 0, 3]).astype(BF16)
            new = (states[s, at].astype(F32) + branch.astype(F32)).astype(BF16)
            states[s + 1, at] = new
            new = new.astype(F32)
            terms.append(new * new)

        @pl.when(s < SECTIONS - 1)
        def _():
            start1(i + chunks, packed(terms))

        @pl.when((i >= 1) & (i <= (SECTIONS - 1) * chunks))
        def _():
            start2(i + chunks - 1)

        return 0

    lax.fori_loop(0, SECTIONS * chunks, forward, 0)

    offset = SECTIONS * chunks

    def backward(j, _):
        s, c = SECTIONS - 1 - j // chunks, chunks - 1 - j % chunks
        base = c * chunk

        @pl.when(j < chunks)
        def _():
            at = span_of(base, chunk)
            cot[at] = states[SECTIONS, at] * valid[at]

        @pl.when(j >= chunks)
        def _():
            along = finish(offset + j - chunks) * (1.0 / width)
            gain = gain_of(s + 1)
            for g in range(groups):
                at = span_of(base + g * GROUP, GROUP)
                wide = scale_x[s + 1, at]
                pulled = grad_normed[at].astype(F32) * gain
                unit = states[s + 1, at].astype(F32) * wide
                fresh = cot[at].astype(F32) + wide * (pulled - unit * spread(along[g : g + 1]))
                cot[at] = fresh.astype(BF16)

        @pl.when(c == chunks - 1)
        def _():
            carry[...] = jnp.zeros_like(carry)

        for g in range(groups):
            at = span_of(base + g * GROUP, GROUP)
            grad_mixed[pl.ds(g * GROUP, GROUP)] = dot_nt(cot[at], weights_ref[s, 0, 3]).astype(BF16)
        whole = span_of(base, chunk)
        sums[s, 3] += dot_tn(mixed[s, whole], cot[whole])

        late_k, late_v = carry[0], carry[1]
        for b in reversed(range(blocks)):
            at = span_of(base + b * SPAN, SPAN)
            near = span_of(base + b * SPAN, 2 * SPAN)
            here = pl.ds(b * SPAN, SPAN)
            gm = grad_mixed[here]
            share = chances[s, c * blocks + b]
            wide_share = share.astype(F32)
            grad_share = dot_nt(gm, values[s, near])
            mean = jnp.sum(grad_share * wide_share, axis=1, keepdims=True)
            grad_score = (wide_share * (grad_share - mean) * (HEAD**-0.5)).astype(BF16)
            qn = queries[s, at]
            unit_v = dot_tn(share, gm)
            unit_k = dot_tn(grad_score, qn)
            unit_q = dot(grad_score, keys[s, near])
            along = dot((unit_q * qn.astype(F32)).astype(BF16), ones)
            grad_q[here] = (scale_q[s, at] * (unit_q - qn.astype(F32) * along)).astype(BF16)
            grad_v[here] = (unit_v[SPAN:] + late_v).astype(BF16)
            mine_k = unit_k[SPAN:] + late_k
            kn = keys[s, span_of(base + b * SPAN + SPAN, SPAN)].astype(F32)
            along = dot((mine_k * kn).astype(BF16), ones)
            grad_k[here] = (scale_k[s, at] * (mine_k - kn * along)).astype(BF16)
            late_k, late_v = unit_k[:SPAN], unit_v[:SPAN]
        carry[0] = late_k
        carry[1] = late_v

        xn = normed[s, whole]
        sums[s, 0] += dot_tn(xn, grad_q[...])
        sums[s, 1] += dot_tn(xn, grad_k[...])
        sums[s, 2] += dot_tn(xn, grad_v[...])

        @pl.when(s > 0)
        def _():
            terms = []
            for g in range(groups):
                at = span_of(base + g * GROUP, GROUP)
                here = pl.ds(g * GROUP, GROUP)
                grad = dot_nt(grad_q[here], weights_ref[s, 0, 0])
                grad = grad + dot_nt(grad_k[here], weights_ref[s, 0, 1])
                grad = grad + dot_nt(grad_v[here], weights_ref[s, 0, 2])
                grad = grad.astype(BF16)
                grad_normed[at] = grad
                terms.append(grad.astype(F32) * normed[s, at].astype(F32))
            start1(offset + j, packed(terms))

        @pl.when((j >= 1) & (j <= (SECTIONS - 1) * chunks))
        def _():
            start2(offset + j - 1)

        return 0

    lax.fori_loop(0, SECTIONS * chunks, backward, 0)

    grads_ref[...] = sums[...].astype(BF16)

    def drain(item, _):
        pltpu.make_async_copy(recv1.at[item], recv1.at[item], send1_sem.at[item]).wait()
        pltpu.make_async_copy(recv2.at[item], recv2.at[item], send2_sem.at[item]).wait()
        return 0

    lax.fori_loop(0, offset + (SECTIONS - 1) * chunks, drain, 0)

    @pl.when(in_window)
    def _():
        def settle(o, _):
            pltpu.make_async_copy(piece(me), piece(me), in_send).wait()
            return 0

        lax.fori_loop(1, seq, settle, 0)


def local(inputs, weights, gains, doc_lengths):
    seq = lax.axis_size("seq")
    total = inputs.shape[2] * seq
    width = gains.shape[1]
    rows = total // 2 + 2 * SPAN
    chunks = 3 if rows % (3 * GROUP) == 0 else 2
    chunk = rows // chunks
    across = 4 if seq > 4 else 2
    down = seq // across
    items = (2 * SECTIONS - 1) * chunks
    cfg = dict(total=total, seq=seq, width=width, across=across, rows=rows, chunk=chunk, chunks=chunks)
    scratch = [
        pltpu.VMEM((SECTIONS + 1, rows, HEAD), BF16),
        pltpu.VMEM((SECTIONS, rows, HEAD), BF16),
        pltpu.VMEM((SECTIONS, rows, HEAD), BF16),
        pltpu.VMEM((SECTIONS, SPAN + rows, HEAD), BF16),
        pltpu.VMEM((SECTIONS, SPAN + rows, HEAD), BF16),
        pltpu.VMEM((SECTIONS, rows, HEAD), BF16),
        pltpu.VMEM((SECTIONS, rows // SPAN, SPAN, 2 * SPAN), BF16),
        pltpu.VMEM((SECTIONS, rows, HEAD), F32),
        pltpu.VMEM((SECTIONS, rows, HEAD), F32),
        pltpu.VMEM((SECTIONS, rows, HEAD), F32),
        pltpu.VMEM((rows // SPAN, SPAN, 2 * SPAN), F32),
        pltpu.VMEM((rows, HEAD), BF16),
        pltpu.VMEM((rows, HEAD), BF16),
        pltpu.VMEM((chunk, HEAD), BF16),
        pltpu.VMEM((rows, HEAD), BF16),
        pltpu.VMEM((chunk, HEAD), BF16),
        pltpu.VMEM((chunk, HEAD), BF16),
        pltpu.VMEM((chunk, HEAD), BF16),
        pltpu.VMEM((2, SPAN, HEAD), F32),
        pltpu.VMEM((SECTIONS, 4, HEAD, HEAD), F32),
        pltpu.VMEM((SECTIONS, 8, HEAD), F32),
        pltpu.VMEM((items, 8, HEAD), F32),
        pltpu.VMEM((items, across - 1, 8, HEAD), F32),
        pltpu.VMEM((items, 8, HEAD), F32),
        pltpu.VMEM((items, down - 1, 8, HEAD), F32),
        pltpu.SemaphoreType.DMA,
        pltpu.SemaphoreType.DMA,
        pltpu.SemaphoreType.DMA((items,)),
        pltpu.SemaphoreType.DMA((items,)),
        pltpu.SemaphoreType.DMA((items,)),
        pltpu.SemaphoreType.DMA((items,)),
    ]
    vmem = pl.BlockSpec(memory_space=pltpu.VMEM)
    grads = pl.pallas_call(
        functools.partial(kernel, cfg),
        out_shape=jax.ShapeDtypeStruct((SECTIONS, 4, HEAD, HEAD), BF16),
        in_specs=[pl.BlockSpec(memory_space=pl.ANY), vmem, vmem, vmem],
        out_specs=vmem,
        scratch_shapes=scratch,
        compiler_params=pltpu.CompilerParams(
            collective_id=0, has_side_effects=True, vmem_limit_bytes=50 * 1024 * 1024
        ),
    )(inputs, weights, gains, doc_lengths)
    own = lax.psum_scatter(grads, "pipe", scatter_dimension=0, tiled=True)
    return lax.psum(own, "dp").astype(F32)[:, None]


def solution(mesh):
    placed = (
        P("dp", None, "seq", None),
        P(None, "seq", None, None, None),
        P(),
        P("dp", None, None),
    )
    return jax.shard_map(
        local,
        mesh=mesh,
        in_specs=placed,
        out_specs=P("pipe", "seq", None, None, None),
        check_vma=False,
    )
```

```python
import functools

import jax
import jax.numpy as jnp
from jax import lax
from jax.experimental import pallas as pl
from jax.experimental.pallas import tpu as pltpu
from jax.sharding import PartitionSpec as P

EPSILON = 1e-06
SECTIONS = 4
SPAN = 64
HEAD = 128
GROUP = 128
F32 = jnp.float32
BF16 = jnp.bfloat16
LOG2E = 1.4426950408889634


def dot(a, b):
    return lax.dot_general(a, b, (((1,), (0,)), ((), ())), preferred_element_type=F32)


def dot_nt(a, b):
    return lax.dot_general(a, b, (((1,), (1,)), ((), ())), preferred_element_type=F32)


def dot_tn(a, b):
    return lax.dot_general(a, b, (((0,), (0,)), ((), ())), preferred_element_type=F32)


def kernel(
    cfg,
    inputs_ref,
    weights_ref,
    gains_ref,
    docs_ref,
    grads_ref,
    weights,
    gains,
    docs,
    weights_in,
    weights_back,
    states,
    normed,
    queries,
    keys,
    values,
    mixed,
    chances,
    scale_q,
    scale_k,
    scale_x,
    mask,
    valid,
    cot,
    grad_normed,
    carry,
    sums,
    gain_rows,
    send1,
    recv1,
    send2,
    recv2,
    half_send,
    half_recv,
    chip_send,
    chip_recv,
    own_send,
    own_recv,
    load_sem,
    in_send,
    in_recv,
    send1_sem,
    recv1_sem,
    send2_sem,
    recv2_sem,
    half_send_sem,
    half_recv_sem,
    chip_send_sem,
    chip_recv_sem,
    own_send_sem,
    own_recv_sem,
):
    total, seq, width, across = cfg["total"], cfg["seq"], cfg["width"], cfg["across"]
    rows, chunk, chunks = cfg["rows"], cfg["chunk"], cfg["chunks"]
    pipe, dp = cfg["pipe"], cfg["dp"]
    down = seq // across
    groups, blocks = chunk // GROUP, chunk // SPAN
    all_blocks = rows // SPAN
    place, me, replica = lax.axis_index("pipe"), lax.axis_index("seq"), lax.axis_index("dp")
    micro, half = place // 2, place % 2
    core = half
    chip = micro * dp + replica
    first_block = half * (seq - all_blocks)
    window = first_block * SPAN
    my_x, my_y = me % across, me // across

    loads = [
        pltpu.make_async_copy(weights_ref.at[:, 0], weights, load_sem.at[0]),
        pltpu.make_async_copy(
            gains_ref.at[:, pl.ds(pl.multiple_of(me * HEAD, HEAD), HEAD)], gains, load_sem.at[1]
        ),
        pltpu.make_async_copy(docs_ref.at[0], docs, load_sem.at[2]),
    ]
    for load in loads:
        load.start()

    barrier = pltpu.get_barrier_semaphore()

    def greet(o, _):
        pl.semaphore_signal(barrier, inc=1, device_id={"seq": (me + o) % seq})
        return 0

    def greet_column(o, _):
        other = (place * dp + replica + o) % (pipe * dp)
        pl.semaphore_signal(barrier, inc=1, device_id={"pipe": other // dp, "dp": other % dp})
        return 0

    lax.fori_loop(1, seq, greet, 0)
    lax.fori_loop(1, pipe * dp, greet_column, 0)
    pl.semaphore_wait(barrier, seq - 1 + pipe * dp - 1)

    slot = me - first_block
    in_window = (slot >= 0) & (slot < all_blocks)

    def piece(head):
        return inputs_ref.at[0, micro, :, pl.ds(pl.multiple_of(head * HEAD, HEAD), HEAD)]

    @pl.when(in_window)
    def _():
        landing = states.at[0, pl.ds(pl.multiple_of(slot * SPAN, SPAN), SPAN)]

        def send(o, _):
            peer = (me + o) % seq
            pltpu.make_async_remote_copy(
                src_ref=piece(peer),
                dst_ref=landing,
                send_sem=in_send,
                recv_sem=in_recv,
                device_id={"seq": peer},
            ).start()
            return 0

        lax.fori_loop(1, seq, send, 0)
        pltpu.make_async_copy(piece(me), landing, in_recv).start()

    ones = jnp.full((HEAD, HEAD), 1.0, BF16)
    mean = jnp.full((HEAD, HEAD), 1.0 / HEAD, BF16)
    row8 = lax.broadcasted_iota(jnp.int32, (8, HEAD), 0)
    row16 = lax.broadcasted_iota(jnp.int32, (16, groups * HEAD), 0) % 8
    lane16 = lax.broadcasted_iota(jnp.int32, (16, groups * HEAD), 1) // HEAD
    selector = jnp.where(row16 == lane16, 1.0, 0.0).astype(BF16)

    for load in loads:
        load.wait()

    both = docs[...].astype(F32)
    lengths = jnp.where(micro == 0, both[0:1], both[1:2]).astype(BF16)
    count = lengths.shape[1]
    earlier = lax.broadcasted_iota(jnp.int32, (count, HEAD), 0) < lax.broadcasted_iota(
        jnp.int32, (count, HEAD), 1
    )
    starts = dot(jnp.broadcast_to(lengths, (8, count)), jnp.where(earlier, 1.0, 0.0).astype(BF16))[:1]
    mid = total // 2

    def make_mask(b, _):
        base = window + b * SPAN
        token = base + lax.broadcasted_iota(jnp.int32, (SPAN, HEAD), 0)
        key = base - SPAN + lax.broadcasted_iota(jnp.int32, (SPAN, HEAD), 1)
        reach = jnp.where(starts <= token.astype(F32), starts, 0.0)
        begin = jnp.max(reach, axis=1, keepdims=True)
        allowed = (key.astype(F32) >= begin) & (key <= token)
        mask[b] = jnp.where(allowed, 1.0, 0.0)
        late = jnp.where(begin >= mid, 1.0, 0.0)
        mine = jnp.where(half == 1, late, 1.0 - late)
        valid[pl.ds(pl.multiple_of(b * SPAN, SPAN), SPAN)] = jnp.broadcast_to(mine, (SPAN, HEAD)).astype(BF16)
        return 0

    lax.fori_loop(0, all_blocks, make_mask, 0)
    for s in range(SECTIONS):
        keys[s, :SPAN] = jnp.zeros((SPAN, HEAD), BF16)
        values[s, :SPAN] = jnp.zeros((SPAN, HEAD), BF16)
        gain_rows[s] = jnp.broadcast_to(gains[s : s + 1], (8, HEAD))
    sums[...] = jnp.zeros_like(sums)

    def arrange(s, _):
        for m in range(4):
            block = weights[s, m]
            if m < 3:
                weights_in[s, :, m * HEAD : (m + 1) * HEAD] = block
            weights_back[s, m * HEAD : (m + 1) * HEAD] = jnp.transpose(block.astype(F32)).astype(BF16)
        return 0

    lax.fori_loop(0, SECTIONS, arrange, 0)

    def packed(term):
        total_rows = None
        for g in range(groups):
            pick = jnp.where(row8 == g, 1.0, 0.0).astype(BF16)
            part = dot_nt(pick, term[g * GROUP : (g + 1) * GROUP])
            total_rows = part if total_rows is None else total_rows + part
        return total_rows

    def spread(packed_rows):
        high = packed_rows.astype(BF16)
        low = (packed_rows - high.astype(F32)).astype(BF16)
        wide = dot_tn(jnp.concatenate([high, low], axis=0), selector)
        return jnp.concatenate([wide[:, g * HEAD : (g + 1) * HEAD] for g in range(groups)], axis=0)

    def start1(item, part):
        send1[item] = part
        for o in range(1, across):
            pltpu.make_async_remote_copy(
                src_ref=send1.at[item],
                dst_ref=recv1.at[item, o - 1],
                send_sem=send1_sem.at[item],
                recv_sem=recv1_sem.at[item],
                device_id={"seq": my_y * across + (my_x + o) % across},
            ).start()

    def start2(item):
        pltpu.make_async_copy(recv1.at[item], recv1.at[item], recv1_sem.at[item]).wait()
        part = send1[item]
        for o in range(across - 1):
            part = part + recv1[item, o]
        send2[item] = part
        for o in range(1, down):
            pltpu.make_async_remote_copy(
                src_ref=send2.at[item],
                dst_ref=recv2.at[item, o - 1],
                send_sem=send2_sem.at[item],
                recv_sem=recv2_sem.at[item],
                device_id={"seq": ((my_y + o) % down) * across + my_x},
            ).start()

    def finish(item):
        pltpu.make_async_copy(recv2.at[item], recv2.at[item], recv2_sem.at[item]).wait()
        part = send2[item]
        for o in range(down - 1):
            part = part + recv2[item, o]
        return part

    def span_of(start, size):
        return pl.ds(pl.multiple_of(start, SPAN), size)

    def gain_of(s):
        return gain_rows[s][:1]

    def cut(value, b, size=SPAN):
        return value[b * SPAN : b * SPAN + size]

    def start_halves(s):
        for m in range(2):
            theirs = jnp.where(core == 0, sums[s, 2 + m], sums[s, m])
            half_send[s, m] = theirs.astype(BF16)
        pltpu.make_async_remote_copy(
            src_ref=half_send.at[s],
            dst_ref=half_recv.at[s],
            send_sem=half_send_sem.at[s],
            recv_sem=half_recv_sem.at[s],
            device_id={"pipe": micro * 2 + 1 - core},
        ).start()

    def start_chips(s):
        pltpu.make_async_copy(half_recv.at[s], half_recv.at[s], half_recv_sem.at[s]).wait()
        for m in range(2):
            ours = jnp.where(core == 0, sums[s, m], sums[s, 2 + m])
            chip_send[s, m] = (ours + half_recv[s, m].astype(F32)).astype(BF16)
        for m in range(2):
            owner = core * 2 + m
            here = (place == s) & (replica == owner)

            @pl.when(here)
            def _():
                pltpu.make_async_copy(chip_send.at[s, m], chip_recv.at[chip], chip_recv_sem).start()

            @pl.when(jnp.logical_not(here))
            def _():
                pltpu.make_async_remote_copy(
                    src_ref=chip_send.at[s, m],
                    dst_ref=chip_recv.at[chip],
                    send_sem=chip_send_sem.at[s],
                    recv_sem=chip_recv_sem,
                    device_id={"pipe": s, "dp": owner},
                ).start()

    def own_sum():
        pltpu.make_async_copy(chip_recv, chip_recv, chip_recv_sem).wait()
        part = chip_recv[0].astype(F32)
        for k in range(1, 2 * dp):
            part = part + chip_recv[k].astype(F32)
        own_send[...] = part.astype(BF16)
        for o in range(1, dp):
            pltpu.make_async_remote_copy(
                src_ref=own_send,
                dst_ref=own_recv.at[o - 1],
                send_sem=own_send_sem,
                recv_sem=own_recv_sem,
                device_id={"dp": (replica + o) % dp},
            ).start()
        grads_ref[0, 0, replica] = part
        pltpu.make_async_copy(own_recv, own_recv, own_recv_sem).wait()
        for o in range(1, dp):
            grads_ref[0, 0, (replica - o + dp) % dp] = own_recv[o - 1].astype(F32)

    pltpu.make_async_copy(states.at[0], states.at[0], in_recv).wait()

    def begin(c, _):
        x = states[0, span_of(c * chunk, chunk)].astype(F32)
        start1(c, packed((x * x).astype(BF16)))
        return 0

    lax.fori_loop(0, chunks, begin, 0)
    lax.fori_loop(0, chunks, lambda c, _: (start2(c), 0)[1], 0)

    def forward(i, _):
        s, c = i // chunks, i % chunks
        base = c * chunk
        whole = span_of(base, chunk)
        padded = span_of(base + SPAN, chunk)
        rs = lax.rsqrt(finish(i) * (1.0 / width) + EPSILON)
        wide = spread(rs)
        x = states[s, whole].astype(F32)
        xn = (x * wide * gain_of(s)).astype(BF16)
        scale_x[s, whole] = wide
        normed[s, whole] = xn
        qkv = dot(xn, weights_in[s])
        q, k = qkv[:, :HEAD], qkv[:, HEAD : 2 * HEAD]
        v = qkv[:, 2 * HEAD :].astype(BF16)
        rq = lax.rsqrt(dot((q * q).astype(BF16), mean) + EPSILON)
        rk = lax.rsqrt(dot((k * k).astype(BF16), mean) + EPSILON)
        qn = (q * rq).astype(BF16)
        kn = (k * rk).astype(BF16)
        scale_q[s, whole] = rq * HEAD**-0.5
        scale_k[s, whole] = rk * HEAD**-0.5
        queries[s, whole] = qn
        near_k = jnp.concatenate([keys[s, span_of(base, SPAN)], kn], axis=0)
        near_v = jnp.concatenate([values[s, span_of(base, SPAN)], v], axis=0)
        keys[s, padded] = kn
        values[s, padded] = v
        scores = [dot_nt(cut(qn, b), cut(near_k, b, 2 * SPAN)) for b in range(blocks)]
        raised = [
            (jnp.exp2(scores[b] * (LOG2E * HEAD**-0.5)) * mask[c * blocks + b]).astype(BF16)
            for b in range(blocks)
        ]
        both = [
            dot(raised[b], jnp.concatenate([cut(near_v, b, 2 * SPAN), ones], axis=1))
            for b in range(blocks)
        ]
        inverse = [1.0 / both[b][:, HEAD:] for b in range(blocks)]
        for b in range(blocks):
            chances[s, c * blocks + b] = (raised[b].astype(F32) * inverse[b]).astype(BF16)
        o = jnp.concatenate([(both[b][:, :HEAD] * inverse[b]).astype(BF16) for b in range(blocks)], axis=0)
        mixed[s, whole] = o
        branch = dot(o, weights[s, 3]).astype(BF16)
        new = (x + branch.astype(F32)).astype(BF16)
        states[s + 1, whole] = new

        @pl.when(s < SECTIONS - 1)
        def _():
            wide_new = new.astype(F32)
            start1(i + chunks, packed((wide_new * wide_new).astype(BF16)))

        @pl.when((i >= 1) & (i <= (SECTIONS - 1) * chunks))
        def _():
            start2(i + chunks - 1)

        return 0

    lax.fori_loop(0, SECTIONS * chunks, forward, 0)

    offset = SECTIONS * chunks

    def backward(j, _):
        s, c = SECTIONS - 1 - j // chunks, chunks - 1 - j % chunks
        base = c * chunk
        whole = span_of(base, chunk)

        @pl.when(j < chunks)
        def _():
            cot[whole] = states[SECTIONS, whole] * valid[whole]

        @pl.when(j >= chunks)
        def _():
            along = spread(finish(offset + j - chunks) * (1.0 / width))
            wide = scale_x[s + 1, whole]
            pulled = grad_normed[whole].astype(F32) * gain_of(s + 1)
            unit = states[s + 1, whole].astype(F32) * wide
            cot[whole] = (cot[whole].astype(F32) + wide * (pulled - unit * along)).astype(BF16)

        @pl.when(c == chunks - 1)
        def _():
            carry[...] = jnp.zeros_like(carry)

        g = cot[whole]
        o = mixed[s, whole]
        gm = dot(g, weights_back[s, 3 * HEAD :]).astype(BF16)
        delta = dot((gm.astype(F32) * o.astype(F32)).astype(BF16), ones)
        near = span_of(base, chunk + SPAN)
        near_k, near_v = keys[s, near], values[s, near]
        qn = queries[s, whole]
        grad_share = [dot_nt(cut(gm, b), cut(near_v, b, 2 * SPAN)) for b in range(blocks)]
        share = [chances[s, c * blocks + b] for b in range(blocks)]
        grad_score = [
            (share[b].astype(F32) * (grad_share[b] - cut(delta, b))).astype(BF16) for b in range(blocks)
        ]
        unit_v = [dot_tn(share[b], cut(gm, b)) for b in range(blocks)]
        unit_q = [dot(grad_score[b], cut(near_k, b, 2 * SPAN)) for b in range(blocks)]
        unit_k = [dot_tn(grad_score[b], cut(qn, b)) for b in range(blocks)]
        late_k = [unit_k[b][:SPAN] for b in range(1, blocks)] + [carry[0]]
        late_v = [unit_v[b][:SPAN] for b in range(1, blocks)] + [carry[1]]
        all_k = jnp.concatenate([unit_k[b][SPAN:] + late_k[b] for b in range(blocks)], axis=0)
        dv = jnp.concatenate([(unit_v[b][SPAN:] + late_v[b]).astype(BF16) for b in range(blocks)], axis=0)
        carry[0] = unit_k[0][:SPAN]
        carry[1] = unit_v[0][:SPAN]
        all_q = jnp.concatenate(unit_q, axis=0)
        wide_q = qn.astype(F32)
        wide_k = near_k[SPAN:].astype(F32)
        along_q = dot((all_q * wide_q).astype(BF16), mean)
        along_k = dot((all_k * wide_k).astype(BF16), mean)
        dq = (scale_q[s, whole] * (all_q - wide_q * along_q)).astype(BF16)
        dk = (scale_k[s, whole] * (all_k - wide_k * along_k)).astype(BF16)
        joined = jnp.concatenate([dq, dk, dv], axis=1)
        xn = normed[s, whole]

        @pl.when(s > 0)
        def _():
            grad = dot(joined, weights_back[s, : 3 * HEAD]).astype(BF16)
            grad_normed[whole] = grad
            start1(offset + j, packed((grad.astype(F32) * xn.astype(F32)).astype(BF16)))

        sums[s, 3] += dot_tn(o, g)
        part = dot_tn(xn, joined)
        for m in range(3):
            sums[s, m] += part[:, m * HEAD : (m + 1) * HEAD]

        @pl.when(c == 0)
        def _():
            start_halves(s)

        @pl.when((j >= 1) & (j <= (SECTIONS - 1) * chunks))
        def _():
            start2(offset + j - 1)

        @pl.when((j >= chunks) & (j % chunks == 0))
        def _():
            start_chips(s + 1)

        return 0

    lax.fori_loop(0, SECTIONS * chunks, backward, 0)

    start_chips(0)
    own_sum()

    def drain(item, _):
        pltpu.make_async_copy(recv1.at[item], recv1.at[item], send1_sem.at[item]).wait()
        pltpu.make_async_copy(recv2.at[item], recv2.at[item], send2_sem.at[item]).wait()
        return 0

    lax.fori_loop(0, offset + (SECTIONS - 1) * chunks, drain, 0)

    def drain_grads(s, _):
        pltpu.make_async_copy(half_send.at[s], half_send.at[s], half_send_sem.at[s]).wait()
        here = (place == s) & (replica // 2 == core)

        @pl.when(here)
        def _():
            pltpu.make_async_copy(chip_send.at[s, 0], chip_send.at[s, 0], chip_send_sem.at[s]).wait()

        @pl.when(jnp.logical_not(here))
        def _():
            pltpu.make_async_copy(chip_send.at[s], chip_send.at[s], chip_send_sem.at[s]).wait()

        return 0

    lax.fori_loop(0, SECTIONS, drain_grads, 0)
    pltpu.make_async_copy(own_recv, own_recv, own_send_sem).wait()

    @pl.when(in_window)
    def _():
        def settle(o, _):
            pltpu.make_async_copy(piece(me), piece(me), in_send).wait()
            return 0

        lax.fori_loop(1, seq, settle, 0)


def local(inputs, weights, gains, doc_lengths):
    seq, pipe, dp = lax.axis_size("seq"), lax.axis_size("pipe"), lax.axis_size("dp")
    total = inputs.shape[2] * seq
    width = gains.shape[1]
    rows = total // 2 + 2 * SPAN
    chunks = 3 if rows % (3 * GROUP) == 0 else 2
    chunk = rows // chunks
    across = 4 if seq > 4 else 2
    down = seq // across
    items = (2 * SECTIONS - 1) * chunks
    cfg = dict(
        total=total,
        seq=seq,
        pipe=pipe,
        dp=dp,
        width=width,
        across=across,
        rows=rows,
        chunk=chunk,
        chunks=chunks,
    )
    scratch = [
        pltpu.VMEM((SECTIONS, 4, HEAD, HEAD), BF16),
        pltpu.VMEM((SECTIONS, HEAD), F32),
        pltpu.VMEM(doc_lengths.shape[1:], jnp.int32),
        pltpu.VMEM((SECTIONS, HEAD, 3 * HEAD), BF16),
        pltpu.VMEM((SECTIONS, 4 * HEAD, HEAD), BF16),
        pltpu.VMEM((SECTIONS + 1, rows, HEAD), BF16),
        pltpu.VMEM((SECTIONS, rows, HEAD), BF16),
        pltpu.VMEM((SECTIONS, rows, HEAD), BF16),
        pltpu.VMEM((SECTIONS, SPAN + rows, HEAD), BF16),
        pltpu.VMEM((SECTIONS, SPAN + rows, HEAD), BF16),
        pltpu.VMEM((SECTIONS, rows, HEAD), BF16),
        pltpu.VMEM((SECTIONS, rows // SPAN, SPAN, 2 * SPAN), BF16),
        pltpu.VMEM((SECTIONS, rows, HEAD), F32),
        pltpu.VMEM((SECTIONS, rows, HEAD), F32),
        pltpu.VMEM((SECTIONS, rows, HEAD), F32),
        pltpu.VMEM((rows // SPAN, SPAN, 2 * SPAN), F32),
        pltpu.VMEM((rows, HEAD), BF16),
        pltpu.VMEM((rows, HEAD), BF16),
        pltpu.VMEM((rows, HEAD), BF16),
        pltpu.VMEM((2, SPAN, HEAD), F32),
        pltpu.VMEM((SECTIONS, 4, HEAD, HEAD), F32),
        pltpu.VMEM((SECTIONS, 8, HEAD), F32),
        pltpu.VMEM((items, 8, HEAD), F32),
        pltpu.VMEM((items, across - 1, 8, HEAD), F32),
        pltpu.VMEM((items, 8, HEAD), F32),
        pltpu.VMEM((items, down - 1, 8, HEAD), F32),
        pltpu.VMEM((SECTIONS, 2, HEAD, HEAD), BF16),
        pltpu.VMEM((SECTIONS, 2, HEAD, HEAD), BF16),
        pltpu.VMEM((SECTIONS, 2, HEAD, HEAD), BF16),
        pltpu.VMEM((2 * dp, HEAD, HEAD), BF16),
        pltpu.VMEM((HEAD, HEAD), BF16),
        pltpu.VMEM((dp - 1, HEAD, HEAD), BF16),
        pltpu.SemaphoreType.DMA((3,)),
        pltpu.SemaphoreType.DMA,
        pltpu.SemaphoreType.DMA,
        pltpu.SemaphoreType.DMA((items,)),
        pltpu.SemaphoreType.DMA((items,)),
        pltpu.SemaphoreType.DMA((items,)),
        pltpu.SemaphoreType.DMA((items,)),
        pltpu.SemaphoreType.DMA((SECTIONS,)),
        pltpu.SemaphoreType.DMA((SECTIONS,)),
        pltpu.SemaphoreType.DMA((SECTIONS,)),
        pltpu.SemaphoreType.DMA,
        pltpu.SemaphoreType.DMA,
        pltpu.SemaphoreType.DMA,
    ]
    hbm = pl.BlockSpec(memory_space=pltpu.HBM)
    return pl.pallas_call(
        functools.partial(kernel, cfg),
        out_shape=jax.ShapeDtypeStruct((1, 1, 4, HEAD, HEAD), F32),
        in_specs=[hbm, hbm, hbm, hbm],
        out_specs=pl.BlockSpec(memory_space=pltpu.VMEM),
        scratch_shapes=scratch,
        compiler_params=pltpu.CompilerParams(
            collective_id=0, has_side_effects=True, vmem_limit_bytes=60 * 1024 * 1024
        ),
    )(inputs, weights, gains, doc_lengths)


def solution(mesh):
    placed = (
        P("dp", None, "seq", None),
        P(None, "seq", None, None, None),
        P(),
        P("dp", None, None),
    )
    return jax.shard_map(
        local,
        mesh=mesh,
        in_specs=placed,
        out_specs=P("pipe", "seq", None, None, None),
        check_vma=False,
    )
```

```python
import functools

import jax
import jax.numpy as jnp
from jax import lax
from jax.experimental import pallas as pl
from jax.experimental.pallas import tpu as pltpu
from jax.sharding import PartitionSpec as P

EPSILON = 1e-06
SECTIONS = 4
SPAN = 64
HEAD = 128
GROUP = 128
F32 = jnp.float32
BF16 = jnp.bfloat16
LOG2E = 1.4426950408889634


def dot(a, b):
    return lax.dot_general(a, b, (((1,), (0,)), ((), ())), preferred_element_type=F32)


def dot_nt(a, b):
    return lax.dot_general(a, b, (((1,), (1,)), ((), ())), preferred_element_type=F32)


def dot_tn(a, b):
    return lax.dot_general(a, b, (((0,), (0,)), ((), ())), preferred_element_type=F32)


def kernel(
    cfg,
    inputs_ref,
    weights_ref,
    gains_ref,
    docs_ref,
    grads_ref,
    weights,
    gains,
    docs,
    weights_in,
    weights_back,
    states,
    normed,
    queries,
    keys,
    values,
    mixed,
    chances,
    scale_q,
    scale_k,
    scale_x,
    mask,
    valid,
    cot,
    base_cot,
    carry,
    sums,
    gain_rows,
    tokens,
    square_send,
    square_recv,
    raw,
    current,
    sent,
    received,
    half_send,
    half_recv,
    chip_send,
    chip_recv,
    own_send,
    own_recv,
    load_sem,
    in_send,
    in_recv,
    square_send_sem,
    square_recv_sem,
    sent_sem,
    received_sem,
    half_send_sem,
    half_recv_sem,
    chip_send_sem,
    chip_recv_sem,
    own_send_sem,
    own_recv_sem,
):
    total, seq, width, across = cfg["total"], cfg["seq"], cfg["width"], cfg["across"]
    rows, chunk, chunks = cfg["rows"], cfg["chunk"], cfg["chunks"]
    pipe, dp = cfg["pipe"], cfg["dp"]
    down = seq // across
    groups, blocks = -(-chunk // GROUP), chunk // SPAN
    all_blocks = rows // SPAN
    place, me, replica = lax.axis_index("pipe"), lax.axis_index("seq"), lax.axis_index("dp")
    micro, half = place // 2, place % 2
    core = half
    chip = micro * dp + replica
    first_block = half * (seq - all_blocks)
    window = first_block * SPAN
    my_x, my_y = me & (across - 1), me // across
    offsets = [(x, y) for y in range(down) for x in range(across)][1:]
    offsets.sort(key=lambda o: -(min(o[0], across - o[0]) + min(o[1], down - o[1])))

    def peer_at(offset):
        return ((my_y + offset[1]) & (down - 1)) * across + ((my_x + offset[0]) & (across - 1))

    loads = [
        pltpu.make_async_copy(weights_ref.at[:, 0], weights, load_sem.at[0]),
        pltpu.make_async_copy(
            gains_ref.at[:, pl.ds(pl.multiple_of(me * HEAD, HEAD), HEAD)], gains, load_sem.at[1]
        ),
        pltpu.make_async_copy(docs_ref.at[0], docs, load_sem.at[2]),
        pltpu.make_async_copy(inputs_ref.at[0, micro], tokens, load_sem.at[3]),
    ]
    for load in loads:
        load.start()

    barrier = pltpu.get_barrier_semaphore()

    for o in range(1, seq):
        pl.semaphore_signal(barrier, inc=1, device_id={"seq": me ^ o})
    for o in range(1, pipe * dp):
        other = (place * dp + replica) ^ o
        pl.semaphore_signal(barrier, inc=1, device_id={"pipe": other // dp, "dp": other % dp})

    slot = me - first_block
    in_window = (slot >= 0) & (slot < all_blocks)

    def piece(head):
        return tokens.at[:, pl.ds(pl.multiple_of(head * HEAD, HEAD), HEAD)]

    ones = jnp.full((HEAD, HEAD), 1.0, BF16)
    mean = jnp.full((HEAD, HEAD), 1.0 / HEAD, BF16)
    row8 = lax.broadcasted_iota(jnp.int32, (8, HEAD), 0)
    row16 = lax.broadcasted_iota(jnp.int32, (16, groups * HEAD), 0) % 8
    lane16 = lax.broadcasted_iota(jnp.int32, (16, groups * HEAD), 1) // HEAD
    selector = jnp.where(row16 == lane16, 1.0, 0.0).astype(BF16)

    for load in loads:
        load.wait()

    both = docs[...].astype(F32)
    lengths = jnp.where(micro == 0, both[0:1], both[1:2]).astype(BF16)
    count = lengths.shape[1]
    earlier = lax.broadcasted_iota(jnp.int32, (count, HEAD), 0) < lax.broadcasted_iota(
        jnp.int32, (count, HEAD), 1
    )
    starts = dot(jnp.broadcast_to(lengths, (8, count)), jnp.where(earlier, 1.0, 0.0).astype(BF16))[:1]
    mid = total // 2

    def make_mask(b, _):
        base = window + b * SPAN
        token = base + lax.broadcasted_iota(jnp.int32, (SPAN, HEAD), 0)
        key = base - SPAN + lax.broadcasted_iota(jnp.int32, (SPAN, HEAD), 1)
        reach = jnp.where(starts <= token.astype(F32), starts, 0.0)
        begin = jnp.max(reach, axis=1, keepdims=True)
        allowed = (key.astype(F32) >= begin) & (key <= token)
        mask[b] = jnp.where(allowed, 1.0, 0.0)
        late = jnp.where(begin >= mid, 1.0, 0.0)
        mine = jnp.where(half == 1, late, 1.0 - late)
        valid[pl.ds(pl.multiple_of(b * SPAN, SPAN), SPAN)] = jnp.broadcast_to(mine, (SPAN, HEAD)).astype(BF16)
        return 0

    lax.fori_loop(0, all_blocks, make_mask, 0)
    for s in range(SECTIONS):
        keys[s, :SPAN] = jnp.zeros((SPAN, HEAD), BF16)
        values[s, :SPAN] = jnp.zeros((SPAN, HEAD), BF16)
        gain_rows[s] = jnp.broadcast_to(gains[s : s + 1], (8, HEAD))
    sums[...] = jnp.zeros_like(sums)
    current[...] = jnp.zeros_like(current)

    def arrange(s, _):
        for m in range(4):
            block = weights[s, m]
            if m < 3:
                weights_in[s, :, m * HEAD : (m + 1) * HEAD] = block
            weights_back[s, m * HEAD : (m + 1) * HEAD] = jnp.transpose(block.astype(F32)).astype(BF16)
        return 0

    lax.fori_loop(0, SECTIONS, arrange, 0)

    squares = jnp.zeros((SPAN, HEAD), F32)
    for h in range(seq):
        feature = tokens[:, h * HEAD : (h + 1) * HEAD].astype(F32)
        squares = squares + feature * feature
    twice = jnp.concatenate([squares, squares], axis=0)
    high = twice.astype(BF16)
    low = (twice - high.astype(F32)).astype(BF16)
    square_send[...] = (dot_nt(ones[:8], high) + dot_nt(ones[:8], low))[:1]

    pl.semaphore_wait(barrier, seq - 1 + pipe * dp - 1)

    @pl.when(in_window)
    def _():
        landing = states.at[0, pl.ds(pl.multiple_of(slot * SPAN, SPAN), SPAN)]
        for offset in offsets:
            peer = peer_at(offset)
            pltpu.make_async_remote_copy(
                src_ref=piece(peer),
                dst_ref=landing,
                send_sem=in_send,
                recv_sem=in_recv,
                device_id={"seq": peer},
            ).start()
        pltpu.make_async_copy(piece(me), landing, in_recv).start()
        for offset in offsets:
            pltpu.make_async_remote_copy(
                src_ref=square_send,
                dst_ref=square_recv.at[slot],
                send_sem=square_send_sem,
                recv_sem=square_recv_sem,
                device_id={"seq": peer_at(offset)},
            ).start()
        pltpu.make_async_copy(square_send, square_recv.at[slot], square_recv_sem).start()

    def packed(term):
        if groups * GROUP > chunk:
            spare = jnp.zeros((groups * GROUP - chunk, HEAD), BF16)
            term = jnp.concatenate([term, spare], axis=0)
        total_rows = None
        for g in range(groups):
            pick = jnp.where(row8 == g, 1.0, 0.0).astype(BF16)
            part = dot_nt(pick, term[g * GROUP : (g + 1) * GROUP])
            total_rows = part if total_rows is None else total_rows + part
        return total_rows

    def spread(packed_rows):
        high = packed_rows.astype(BF16)
        low = (packed_rows - high.astype(F32)).astype(BF16)
        wide = dot_tn(jnp.concatenate([high, low], axis=0), selector)
        parts = [wide[:, g * HEAD : (g + 1) * HEAD] for g in range(groups)]
        return jnp.concatenate(parts, axis=0)[:chunk]

    def start(item, part):
        sent[item] = part[:groups]
        for n, offset in enumerate(offsets):
            pltpu.make_async_remote_copy(
                src_ref=sent.at[item],
                dst_ref=received.at[item, n],
                send_sem=sent_sem.at[item],
                recv_sem=received_sem.at[item],
                device_id={"seq": peer_at(offset)},
            ).start()

    def finish(item):
        pltpu.make_async_copy(received.at[item], received.at[item], received_sem.at[item]).wait()
        parts = [sent[item]] + [received[item, n] for n in range(seq - 1)]
        while len(parts) > 1:
            parts = [a + b for a, b in zip(parts[::2], parts[1::2])]
        spare = jnp.zeros((8 - groups, HEAD), F32)
        return jnp.concatenate([parts[0], spare], axis=0) if groups < 8 else parts[0]

    def span_of(start, size):
        return pl.ds(pl.multiple_of(start, SPAN), size)

    def gain_of(s):
        return gain_rows[s][:1]

    def cut(value, b, size=SPAN):
        return value[b * SPAN : b * SPAN + size]

    def start_halves(s):
        for m in range(2):
            theirs = jnp.where(core == 0, sums[s, 2 + m], sums[s, m])
            half_send[s, m] = theirs.astype(BF16)
        pltpu.make_async_remote_copy(
            src_ref=half_send.at[s],
            dst_ref=half_recv.at[s],
            send_sem=half_send_sem.at[s],
            recv_sem=half_recv_sem.at[s],
            device_id={"pipe": micro * 2 + 1 - core},
        ).start()

    def start_chips(s):
        pltpu.make_async_copy(half_recv.at[s], half_recv.at[s], half_recv_sem.at[s]).wait()
        for m in range(2):
            ours = jnp.where(core == 0, sums[s, m], sums[s, 2 + m])
            chip_send[s, m] = (ours + half_recv[s, m].astype(F32)).astype(BF16)
        for m in range(2):
            owner = core * 2 + m
            here = (place == s) & (replica == owner)

            @pl.when(here)
            def _():
                pltpu.make_async_copy(chip_send.at[s, m], chip_recv.at[chip], chip_recv_sem).start()

            @pl.when(jnp.logical_not(here))
            def _():
                pltpu.make_async_remote_copy(
                    src_ref=chip_send.at[s, m],
                    dst_ref=chip_recv.at[chip],
                    send_sem=chip_send_sem.at[s],
                    recv_sem=chip_recv_sem,
                    device_id={"pipe": s, "dp": owner},
                ).start()

    def own_sum():
        pltpu.make_async_copy(chip_recv, chip_recv, chip_recv_sem).wait()
        part = chip_recv[0].astype(F32)
        for k in range(1, 2 * dp):
            part = part + chip_recv[k].astype(F32)
        own_send[...] = part.astype(BF16)
        for o in range(1, dp):
            pltpu.make_async_remote_copy(
                src_ref=own_send,
                dst_ref=own_recv.at[o - 1],
                send_sem=own_send_sem,
                recv_sem=own_recv_sem,
                device_id={"dp": (replica + o) % dp},
            ).start()
        grads_ref[0, 0, replica] = part
        pltpu.make_async_copy(own_recv, own_recv, own_recv_sem).wait()
        for o in range(1, dp):
            grads_ref[0, 0, (replica - o + dp) % dp] = own_recv[o - 1].astype(F32)

    def project(s, c, x):
        qkv = dot((x * gain_of(s)).astype(BF16), weights_in[s])
        q, k = qkv[:, :HEAD], qkv[:, HEAD : 2 * HEAD]
        raw[c, 0], raw[c, 1], raw[c, 2] = q, k, qkv[:, 2 * HEAD :]
        raw[c, 3] = dot((q * q).astype(BF16), mean)
        raw[c, 4] = dot((k * k).astype(BF16), mean)

    pltpu.make_async_copy(states.at[0], states.at[0], in_recv).wait()

    def begin(c, _):
        project(0, c, states[0, span_of(c * chunk, chunk)].astype(F32))
        return 0

    lax.fori_loop(0, chunks, begin, 0)
    pltpu.make_async_copy(square_recv, square_recv, square_recv_sem).wait()

    def forward(i, _):
        s, c = i // chunks, i % chunks
        base = c * chunk
        whole = span_of(base, chunk)
        padded = span_of(base + SPAN, chunk)

        @pl.when(i < chunks)
        def _():
            left = lax.broadcasted_iota(jnp.int32, (1, HEAD), 1) < SPAN
            for g in range(groups):
                first = c * blocks + 2 * g
                second = c * blocks + min(2 * g + 1, blocks - 1)
                current[g : g + 1] = jnp.where(left, square_recv[first], square_recv[second])

        @pl.when(i >= chunks)
        def _():
            current[...] = finish(i - chunks)

        wide = spread(lax.rsqrt(current[...] * (1.0 / width) + EPSILON))
        squared = wide * wide
        x = states[s, whole].astype(F32)
        rq = lax.rsqrt(squared * raw[c, 3] + EPSILON)
        rk = lax.rsqrt(squared * raw[c, 4] + EPSILON)
        qn = (raw[c, 0] * (wide * rq)).astype(BF16)
        kn = (raw[c, 1] * (wide * rk)).astype(BF16)
        v = (raw[c, 2] * wide).astype(BF16)
        near_k = jnp.concatenate([keys[s, span_of(base, SPAN)], kn], axis=0)
        near_v = jnp.concatenate([values[s, span_of(base, SPAN)], v], axis=0)
        scores = [dot_nt(cut(qn, b), cut(near_k, b, 2 * SPAN)) for b in range(blocks)]
        raised = [
            (jnp.exp2(scores[b] * (LOG2E * HEAD**-0.5)) * mask[c * blocks + b]).astype(BF16)
            for b in range(blocks)
        ]
        both = [
            dot(raised[b], jnp.concatenate([cut(near_v, b, 2 * SPAN), ones], axis=1))
            for b in range(blocks)
        ]
        inverse = [1.0 / both[b][:, HEAD:] for b in range(blocks)]
        o = jnp.concatenate([(both[b][:, :HEAD] * inverse[b]).astype(BF16) for b in range(blocks)], axis=0)
        branch = dot(o, weights[s, 3]).astype(BF16)
        new = (x + branch.astype(F32)).astype(BF16)
        wide_new = new.astype(F32)
        states[s + 1, whole] = new
        scale_x[s, whole] = wide
        scale_q[s, whole] = rq * HEAD**-0.5
        scale_k[s, whole] = rk * HEAD**-0.5
        queries[s, whole] = qn
        keys[s, padded] = kn
        values[s, padded] = v
        mixed[s, whole] = o
        for b in range(blocks):
            chances[s, c * blocks + b] = (raised[b].astype(F32) * inverse[b]).astype(BF16)

        @pl.when(s < SECTIONS - 1)
        def _():
            start(i, packed((wide_new * wide_new).astype(BF16)))
            project(s + 1, c, wide_new)

        normed[s, whole] = (x * wide * gain_of(s)).astype(BF16)
        return 0

    lax.fori_loop(0, SECTIONS * chunks, forward, 0)

    later = (SECTIONS - 1) * chunks

    def backward(j, _):
        s, c = SECTIONS - 1 - j // chunks, chunks - 1 - j % chunks
        base = c * chunk
        whole = span_of(base, chunk)

        @pl.when(j < chunks)
        def _():
            cot[whole] = states[SECTIONS, whole] * valid[whole]

        @pl.when(j >= chunks)
        def _():
            along = spread(finish(later + j - chunks) * (1.0 / width))
            wide = scale_x[s + 1, whole]
            unit = states[s + 1, whole].astype(F32) * (wide * wide)
            cot[whole] = (base_cot[whole] - unit * along).astype(BF16)

        @pl.when(c == chunks - 1)
        def _():
            carry[...] = jnp.zeros_like(carry)

        g = cot[whole]
        o = mixed[s, whole]
        gm = dot(g, weights_back[s, 3 * HEAD :]).astype(BF16)
        delta = dot((gm.astype(F32) * o.astype(F32)).astype(BF16), ones)
        near = span_of(base, chunk + SPAN)
        near_k, near_v = keys[s, near], values[s, near]
        qn = queries[s, whole]
        grad_share = [dot_nt(cut(gm, b), cut(near_v, b, 2 * SPAN)) for b in range(blocks)]
        share = [chances[s, c * blocks + b] for b in range(blocks)]
        grad_score = [
            (share[b].astype(F32) * (grad_share[b] - cut(delta, b))).astype(BF16) for b in range(blocks)
        ]
        unit_v = [dot_tn(share[b], cut(gm, b)) for b in range(blocks)]
        unit_q = [dot(grad_score[b], cut(near_k, b, 2 * SPAN)) for b in range(blocks)]
        unit_k = [dot_tn(grad_score[b], cut(qn, b)) for b in range(blocks)]
        late_k = [unit_k[b][:SPAN] for b in range(1, blocks)] + [carry[0]]
        late_v = [unit_v[b][:SPAN] for b in range(1, blocks)] + [carry[1]]
        all_v = jnp.concatenate([unit_v[b][SPAN:] + late_v[b] for b in range(blocks)], axis=0)
        all_k = jnp.concatenate([unit_k[b][SPAN:] + late_k[b] for b in range(blocks)], axis=0)
        dv = all_v.astype(BF16)
        carry[0] = unit_k[0][:SPAN]
        carry[1] = unit_v[0][:SPAN]
        all_q = jnp.concatenate(unit_q, axis=0)
        wide_q = qn.astype(F32)
        wide_k = near_k[SPAN:].astype(F32)
        terms_q = all_q * wide_q
        terms_k = all_k * wide_k
        sq, sk = scale_q[s, whole], scale_k[s, whole]

        @pl.when(s > 0)
        def _():
            small = (EPSILON * HEAD**0.5) * (sq * sq * terms_q + sk * sk * terms_k)
            start(later + j, packed((all_v * near_v[SPAN:].astype(F32) + small).astype(BF16)))

        along_q = dot(terms_q.astype(BF16), mean)
        along_k = dot(terms_k.astype(BF16), mean)
        dq = (sq * (all_q - wide_q * along_q)).astype(BF16)
        dk = (sk * (all_k - wide_k * along_k)).astype(BF16)
        joined = jnp.concatenate([dq, dk, dv], axis=1)
        xn = normed[s, whole]
        grad = dot(joined, weights_back[s, : 3 * HEAD]).astype(BF16)
        base_cot[whole] = g.astype(F32) + scale_x[s, whole] * (grad.astype(F32) * gain_of(s))
        sums[s, 3] += dot_tn(o, g)
        part = dot_tn(xn, joined)
        for m in range(3):
            sums[s, m] += part[:, m * HEAD : (m + 1) * HEAD]

        @pl.when(c == 0)
        def _():
            start_halves(s)

        @pl.when((j >= chunks) & (j % chunks == 0))
        def _():
            start_chips(s + 1)

        return 0

    lax.fori_loop(0, SECTIONS * chunks, backward, 0)

    start_chips(0)
    own_sum()

    def drain(item, _):
        pltpu.make_async_copy(received.at[item], received.at[item], sent_sem.at[item]).wait()
        return 0

    lax.fori_loop(0, 2 * later, drain, 0)

    def drain_grads(s, _):
        pltpu.make_async_copy(half_send.at[s], half_send.at[s], half_send_sem.at[s]).wait()
        here = (place == s) & (replica // 2 == core)

        @pl.when(here)
        def _():
            pltpu.make_async_copy(chip_send.at[s, 0], chip_send.at[s, 0], chip_send_sem.at[s]).wait()

        @pl.when(jnp.logical_not(here))
        def _():
            pltpu.make_async_copy(chip_send.at[s], chip_send.at[s], chip_send_sem.at[s]).wait()

        return 0

    lax.fori_loop(0, SECTIONS, drain_grads, 0)
    pltpu.make_async_copy(own_recv, own_recv, own_send_sem).wait()

    @pl.when(in_window)
    def _():
        def settle(o, _):
            pltpu.make_async_copy(piece(me), piece(me), in_send).wait()
            pltpu.make_async_copy(square_send, square_send, square_send_sem).wait()
            return 0

        lax.fori_loop(1, seq, settle, 0)


def local(inputs, weights, gains, doc_lengths):
    seq, pipe, dp = lax.axis_size("seq"), lax.axis_size("pipe"), lax.axis_size("dp")
    total = inputs.shape[2] * seq
    width = gains.shape[1]
    rows = total // 2 + 2 * SPAN
    chunks = 2
    chunk = rows // chunks
    across = 4 if seq > 4 else 2
    down = seq // across
    items = 2 * (SECTIONS - 1) * chunks
    groups = -(-chunk // GROUP)
    cfg = dict(
        total=total,
        seq=seq,
        pipe=pipe,
        dp=dp,
        width=width,
        across=across,
        rows=rows,
        chunk=chunk,
        chunks=chunks,
    )
    scratch = [
        pltpu.VMEM((SECTIONS, 4, HEAD, HEAD), BF16),
        pltpu.VMEM((SECTIONS, HEAD), F32),
        pltpu.VMEM(doc_lengths.shape[1:], jnp.int32),
        pltpu.VMEM((SECTIONS, HEAD, 3 * HEAD), BF16),
        pltpu.VMEM((SECTIONS, 4 * HEAD, HEAD), BF16),
        pltpu.VMEM((SECTIONS + 1, rows, HEAD), BF16),
        pltpu.VMEM((SECTIONS, rows, HEAD), BF16),
        pltpu.VMEM((SECTIONS, rows, HEAD), BF16),
        pltpu.VMEM((SECTIONS, SPAN + rows, HEAD), BF16),
        pltpu.VMEM((SECTIONS, SPAN + rows, HEAD), BF16),
        pltpu.VMEM((SECTIONS, rows, HEAD), BF16),
        pltpu.VMEM((SECTIONS, rows // SPAN, SPAN, 2 * SPAN), BF16),
        pltpu.VMEM((SECTIONS, rows, HEAD), F32),
        pltpu.VMEM((SECTIONS, rows, HEAD), F32),
        pltpu.VMEM((SECTIONS, rows, HEAD), F32),
        pltpu.VMEM((rows // SPAN, SPAN, 2 * SPAN), F32),
        pltpu.VMEM((rows, HEAD), BF16),
        pltpu.VMEM((rows, HEAD), BF16),
        pltpu.VMEM((rows, HEAD), F32),
        pltpu.VMEM((2, SPAN, HEAD), F32),
        pltpu.VMEM((SECTIONS, 4, HEAD, HEAD), F32),
        pltpu.VMEM((SECTIONS, 8, HEAD), F32),
        pltpu.VMEM((SPAN, width), BF16),
        pltpu.VMEM((1, HEAD), F32),
        pltpu.VMEM((rows // SPAN, 1, HEAD), F32),
        pltpu.VMEM((chunks, 5, chunk, HEAD), F32),
        pltpu.VMEM((8, HEAD), F32),
        pltpu.VMEM((items, groups, HEAD), F32),
        pltpu.VMEM((items, seq - 1, groups, HEAD), F32),
        pltpu.VMEM((SECTIONS, 2, HEAD, HEAD), BF16),
        pltpu.VMEM((SECTIONS, 2, HEAD, HEAD), BF16),
        pltpu.VMEM((SECTIONS, 2, HEAD, HEAD), BF16),
        pltpu.VMEM((2 * dp, HEAD, HEAD), BF16),
        pltpu.VMEM((HEAD, HEAD), BF16),
        pltpu.VMEM((dp - 1, HEAD, HEAD), BF16),
        pltpu.SemaphoreType.DMA((4,)),
        pltpu.SemaphoreType.DMA,
        pltpu.SemaphoreType.DMA,
        pltpu.SemaphoreType.DMA,
        pltpu.SemaphoreType.DMA,
        pltpu.SemaphoreType.DMA((items,)),
        pltpu.SemaphoreType.DMA((items,)),
        pltpu.SemaphoreType.DMA((SECTIONS,)),
        pltpu.SemaphoreType.DMA((SECTIONS,)),
        pltpu.SemaphoreType.DMA((SECTIONS,)),
        pltpu.SemaphoreType.DMA,
        pltpu.SemaphoreType.DMA,
        pltpu.SemaphoreType.DMA,
    ]
    hbm = pl.BlockSpec(memory_space=pltpu.HBM)
    return pl.pallas_call(
        functools.partial(kernel, cfg),
        out_shape=jax.ShapeDtypeStruct((1, 1, 4, HEAD, HEAD), F32),
        in_specs=[hbm, hbm, hbm, hbm],
        out_specs=pl.BlockSpec(memory_space=pltpu.VMEM),
        scratch_shapes=scratch,
        compiler_params=pltpu.CompilerParams(
            collective_id=0, has_side_effects=True, vmem_limit_bytes=60 * 1024 * 1024
        ),
    )(inputs, weights, gains, doc_lengths)


def solution(mesh):
    placed = (
        P("dp", None, "seq", None),
        P(None, "seq", None, None, None),
        P(),
        P("dp", None, None),
    )
    return jax.shard_map(
        local,
        mesh=mesh,
        in_specs=placed,
        out_specs=P("pipe", "seq", None, None, None),
        check_vma=False,
    )
```

```python
import functools

import jax
import jax.numpy as jnp
from jax import lax
from jax.experimental import pallas as pl
from jax.experimental.pallas import tpu as pltpu
from jax.sharding import PartitionSpec as P

EPSILON = 1e-06
EXTRA = 16
SECTIONS = 4
SPAN = 64
HEAD = 128
GROUP = 128
F32 = jnp.float32
BF16 = jnp.bfloat16
LOG2E = 1.4426950408889634


def dot(a, b):
    return lax.dot_general(a, b, (((1,), (0,)), ((), ())), preferred_element_type=F32)


def dot_nt(a, b):
    return lax.dot_general(a, b, (((1,), (1,)), ((), ())), preferred_element_type=F32)


def dot_tn(a, b):
    return lax.dot_general(a, b, (((0,), (0,)), ((), ())), preferred_element_type=F32)


def kernel(
    cfg,
    inputs_ref,
    weights_ref,
    gains_ref,
    docs_ref,
    grads_ref,
    weights,
    gains,
    docs,
    weights_in,
    weights_back,
    states,
    normed,
    queries,
    keys,
    values,
    mixed,
    chances,
    scale_q,
    scale_k,
    scale_x,
    mask,
    valid,
    cot,
    base_cot,
    carry,
    sums,
    gain_rows,
    tokens,
    landing,
    raw,
    current,
    sent,
    received,
    half_send,
    half_recv,
    chip_send,
    chip_recv,
    own_send,
    own_recv,
    load_sem,
    in_send,
    in_recv,
    sent_sem,
    received_sem,
    half_send_sem,
    half_recv_sem,
    chip_send_sem,
    chip_recv_sem,
    own_send_sem,
    own_recv_sem,
):
    total, seq, width, across = cfg["total"], cfg["seq"], cfg["width"], cfg["across"]
    rows, chunk, chunks = cfg["rows"], cfg["chunk"], cfg["chunks"]
    pipe, dp = cfg["pipe"], cfg["dp"]
    down = seq // across
    groups, blocks = -(-chunk // GROUP), chunk // SPAN
    all_blocks = rows // SPAN
    place, me, replica = lax.axis_index("pipe"), lax.axis_index("seq"), lax.axis_index("dp")
    micro, half = place >> 1, place & 1
    core = half
    chip = micro * dp + replica
    first_block = half * (seq - all_blocks)
    window = first_block * SPAN
    my_x, my_y = me & (across - 1), me >> (across.bit_length() - 1)
    offsets = [(x, y) for y in range(down) for x in range(across)][1:]
    offsets.sort(key=lambda o: -(min(o[0], across - o[0]) + min(o[1], down - o[1])))

    def peer_at(offset):
        return ((my_y + offset[1]) & (down - 1)) * across + ((my_x + offset[0]) & (across - 1))

    loads = [
        pltpu.make_async_copy(weights_ref.at[:, 0], weights, load_sem.at[0]),
        pltpu.make_async_copy(
            gains_ref.at[:, pl.ds(pl.multiple_of(me * HEAD, HEAD), HEAD)], gains, load_sem.at[1]
        ),
        pltpu.make_async_copy(docs_ref.at[0], docs, load_sem.at[2]),
        pltpu.make_async_copy(inputs_ref.at[0, micro], tokens.at[pl.ds(0, SPAN)], load_sem.at[3]),
    ]
    for load in loads:
        load.start()

    barrier = pltpu.get_barrier_semaphore()

    distant = [o for o in offsets if min(o[0], across - o[0]) + min(o[1], down - o[1]) > 3]
    close = offsets[len(distant) :]
    for offset in distant:
        pl.semaphore_signal(barrier, inc=1, device_id={"seq": peer_at(offset)})
    for q in range(pipe):
        for r in range(dp):
            if q or r:
                there = {"pipe": place ^ q, "dp": replica ^ r}
                pl.semaphore_signal(barrier, inc=1, device_id=there)
    for offset in close:
        pl.semaphore_signal(barrier, inc=1, device_id={"seq": peer_at(offset)})

    slot = me - first_block
    own_blocks = seq // 2
    lead = all_blocks - own_blocks
    in_window = (slot >= half * lead) & (slot < own_blocks + 1 + half * (all_blocks - own_blocks - 1))
    part = jnp.where(slot >= blocks, 1, 0)

    def piece(head):
        return tokens.at[:, pl.ds(pl.multiple_of(head * HEAD, HEAD), HEAD)]

    later = (SECTIONS - 1) * chunks
    ones = jnp.full((HEAD, HEAD), 1.0, BF16)
    mean = jnp.full((HEAD, HEAD), 1.0 / HEAD, BF16)
    row8 = lax.broadcasted_iota(jnp.int32, (8, HEAD), 0)
    row16 = lax.broadcasted_iota(jnp.int32, (16, groups * HEAD), 0) % 8
    lane16 = lax.broadcasted_iota(jnp.int32, (16, groups * HEAD), 1) // HEAD
    selector = jnp.where(row16 == lane16, 1.0, 0.0).astype(BF16)

    for load in loads:
        load.wait()

    both = docs[...].astype(F32)
    lengths = jnp.where(micro == 0, both[0:1], both[1:2]).astype(BF16)
    count = lengths.shape[1]
    earlier = lax.broadcasted_iota(jnp.int32, (count, HEAD), 0) < lax.broadcasted_iota(
        jnp.int32, (count, HEAD), 1
    )
    starts = dot(jnp.broadcast_to(lengths, (8, count)), jnp.where(earlier, 1.0, 0.0).astype(BF16))[:1]
    mid = total // 2

    def prepare():
        def make_mask(b, _):
            base = window + b * SPAN
            token = base + lax.broadcasted_iota(jnp.int32, (SPAN, HEAD), 0)
            key = base - SPAN + lax.broadcasted_iota(jnp.int32, (SPAN, HEAD), 1)
            reach = jnp.where(starts <= token.astype(F32), starts, 0.0)
            begin = jnp.max(reach, axis=1, keepdims=True)
            allowed = (key.astype(F32) >= begin) & (key <= token)
            mask[b] = jnp.where(allowed, 1.0, 0.0)
            late = jnp.where(begin >= mid, 1.0, 0.0)
            mine = jnp.where(half == 1, late, 1.0 - late)
            valid[pl.ds(pl.multiple_of(b * SPAN, SPAN), SPAN)] = jnp.broadcast_to(mine, (SPAN, HEAD)).astype(BF16)
            return 0

        lax.fori_loop(0, all_blocks, make_mask, 0)
        for s in range(SECTIONS):
            keys[s, :SPAN] = jnp.zeros((SPAN, HEAD), BF16)
            values[s, :SPAN] = jnp.zeros((SPAN, HEAD), BF16)
            gain_rows[s] = jnp.broadcast_to(gains[s : s + 1], (8, HEAD))
        sums[...] = jnp.zeros_like(sums)

        @pl.when(half == 0)
        def _():
            landing[own_blocks + 1 :] = jnp.zeros((all_blocks - own_blocks - 1, SPAN + EXTRA, HEAD), BF16)

        @pl.when(half == 1)
        def _():
            landing[:lead] = jnp.zeros((lead, SPAN + EXTRA, HEAD), BF16)

        current[...] = jnp.zeros_like(current)

        def arrange(s, _):
            for m in range(4):
                block = weights[s, m]
                if m < 3:
                    weights_in[s, :, m * HEAD : (m + 1) * HEAD] = block
                weights_back[s, m * HEAD : (m + 1) * HEAD] = jnp.transpose(block.astype(F32)).astype(BF16)
            return 0

        lax.fori_loop(0, SECTIONS, arrange, 0)

    squares = jnp.zeros((SPAN, HEAD), F32)
    for h in range(seq):
        feature = tokens[:SPAN, h * HEAD : (h + 1) * HEAD].astype(F32)
        squares = squares + feature * feature
    twice = jnp.concatenate([squares, squares], axis=0)
    high = twice.astype(BF16)
    low = (twice - high.astype(F32)).astype(BF16)
    sum_row = (dot_nt(ones[:8], high) + dot_nt(ones[:8], low))[:1]
    high = sum_row.astype(BF16)
    low = (sum_row - high.astype(F32)).astype(BF16)
    extra = jnp.concatenate([high, low, jnp.zeros((EXTRA - 2, HEAD), BF16)], axis=0)
    for h in range(seq):
        tokens[SPAN:, h * HEAD : (h + 1) * HEAD] = extra

    early = (part == 0) & in_window

    @pl.when(early)
    def _():
        prepare()

    pl.semaphore_wait(barrier, seq - 1 + pipe * dp - 1)

    @pl.when(jnp.logical_not(early))
    def _():
        prepare()

    @pl.when(in_window)
    def _():
        for offset in offsets:
            peer = peer_at(offset)
            pltpu.make_async_remote_copy(
                src_ref=piece(peer),
                dst_ref=landing.at[slot],
                send_sem=in_send,
                recv_sem=in_recv.at[part],
                device_id={"seq": peer},
            ).start()
        pltpu.make_async_copy(piece(me), landing.at[slot], in_recv.at[part]).start()

    def packed(term):
        if groups * GROUP > chunk:
            spare = jnp.zeros((groups * GROUP - chunk, HEAD), BF16)
            term = jnp.concatenate([term, spare], axis=0)
        total_rows = None
        for g in range(groups):
            pick = jnp.where(row8 == g, 1.0, 0.0).astype(BF16)
            part = dot_nt(pick, term[g * GROUP : (g + 1) * GROUP])
            total_rows = part if total_rows is None else total_rows + part
        return total_rows

    def spread(packed_rows):
        high = packed_rows.astype(BF16)
        low = (packed_rows - high.astype(F32)).astype(BF16)
        wide = dot_tn(jnp.concatenate([high, low], axis=0), selector)
        parts = [wide[:, g * HEAD : (g + 1) * HEAD] for g in range(groups)]
        return jnp.concatenate(parts, axis=0)[:chunk]

    def start(item, part):
        sent[item] = part[:groups]
        for n, offset in enumerate(offsets):
            pltpu.make_async_remote_copy(
                src_ref=sent.at[item],
                dst_ref=received.at[item, n],
                send_sem=sent_sem.at[item],
                recv_sem=received_sem.at[item],
                device_id={"seq": peer_at(offset)},
            ).start()

    def finish(item):
        pltpu.make_async_copy(received.at[item], received.at[item], received_sem.at[item]).wait()
        parts = [sent[item]] + [received[item, n] for n in range(seq - 1)]
        while len(parts) > 1:
            parts = [a + b for a, b in zip(parts[::2], parts[1::2])]
        spare = jnp.zeros((8 - groups, HEAD), F32)
        return jnp.concatenate([parts[0], spare], axis=0) if groups < 8 else parts[0]

    def span_of(start, size):
        return pl.ds(pl.multiple_of(start, SPAN), size)

    def gain_of(s):
        return gain_rows[s][:1]

    def cut(value, b, size=SPAN):
        return value[b * SPAN : b * SPAN + size]

    def start_halves(s):
        for m in range(2):
            theirs = jnp.where(core == 0, sums[s, 2 + m], sums[s, m])
            half_send[s, m] = theirs.astype(BF16)
        pltpu.make_async_remote_copy(
            src_ref=half_send.at[s],
            dst_ref=half_recv.at[s],
            send_sem=half_send_sem.at[s],
            recv_sem=half_recv_sem.at[s],
            device_id={"pipe": micro * 2 + 1 - core},
        ).start()

    def start_chips(s):
        pltpu.make_async_copy(half_recv.at[s], half_recv.at[s], half_recv_sem.at[s]).wait()
        for m in range(2):
            ours = jnp.where(core == 0, sums[s, m], sums[s, 2 + m])
            chip_send[s, m] = (ours + half_recv[s, m].astype(F32)).astype(BF16)
        for m in range(2):
            owner = core * 2 + m
            here = (place == s) & (replica == owner)

            @pl.when(here)
            def _():
                pltpu.make_async_copy(chip_send.at[s, m], chip_recv.at[chip], chip_recv_sem).start()

            @pl.when(jnp.logical_not(here))
            def _():
                pltpu.make_async_remote_copy(
                    src_ref=chip_send.at[s, m],
                    dst_ref=chip_recv.at[chip],
                    send_sem=chip_send_sem.at[s],
                    recv_sem=chip_recv_sem,
                    device_id={"pipe": s, "dp": owner},
                ).start()

    def drain():
        def drain_item(item, _):
            pltpu.make_async_copy(received.at[item], received.at[item], sent_sem.at[item]).wait()
            return 0

        lax.fori_loop(0, 2 * later, drain_item, 0)

        def drain_grads(s, _):
            pltpu.make_async_copy(half_send.at[s], half_send.at[s], half_send_sem.at[s]).wait()
            here = (place == s) & (replica // 2 == core)

            @pl.when(here)
            def _():
                pltpu.make_async_copy(chip_send.at[s, 0], chip_send.at[s, 0], chip_send_sem.at[s]).wait()

            @pl.when(jnp.logical_not(here))
            def _():
                pltpu.make_async_copy(chip_send.at[s], chip_send.at[s], chip_send_sem.at[s]).wait()

            return 0

        lax.fori_loop(0, SECTIONS, drain_grads, 0)

        @pl.when(in_window)
        def _():
            all_sent = tokens.at[:, pl.ds(0, (seq - 1) * HEAD)]
            pltpu.make_async_copy(all_sent, all_sent, in_send).wait()

    def own_sum():
        pltpu.make_async_copy(chip_recv, chip_recv, chip_recv_sem).wait()
        part = chip_recv[0].astype(F32)
        for k in range(1, 2 * dp):
            part = part + chip_recv[k].astype(F32)
        own_send[...] = part.astype(BF16)
        for o in range(1, dp):
            pltpu.make_async_remote_copy(
                src_ref=own_send,
                dst_ref=own_recv.at[o - 1],
                send_sem=own_send_sem,
                recv_sem=own_recv_sem,
                device_id={"dp": (replica + o) % dp},
            ).start()
        grads_ref[0, 0, replica] = own_send[...]
        drain()
        pltpu.make_async_copy(own_recv, own_recv, own_recv_sem).wait()
        for o in range(1, dp):
            grads_ref[0, 0, (replica - o + dp) % dp] = own_recv[o - 1]
        pltpu.make_async_copy(own_recv, own_recv, own_send_sem).wait()

    def project(s, c, x):
        qkv = dot((x * gain_of(s)).astype(BF16), weights_in[s])
        q, k = qkv[:, :HEAD], qkv[:, HEAD : 2 * HEAD]
        raw[c, 0], raw[c, 1], raw[c, 2] = q, k, qkv[:, 2 * HEAD :]
        raw[c, 3] = dot((q * q).astype(BF16), mean)
        raw[c, 4] = dot((k * k).astype(BF16), mean)

    def arrived(c):
        for h in range(2):
            first = max(c * blocks, lead if h else 0)
            last = min((c + 1) * blocks, all_blocks if h else own_blocks + 1)

            @pl.when(half == h)
            def _():
                there = landing.at[pl.ds(first, last - first)]
                pltpu.make_async_copy(there, there, in_recv.at[c]).wait()

    def forward(i, _):
        s, c = i // chunks, i % chunks
        base = c * chunk
        whole = span_of(base, chunk)
        padded = span_of(base + SPAN, chunk)

        for k in range(chunks):
            @pl.when(i == k)
            def _():
                arrived(k)

        @pl.when(i < chunks)
        def _():
            new = jnp.concatenate([landing[c * blocks + b, :SPAN] for b in range(blocks)], axis=0)
            states[0, whole] = new
            project(0, c, new.astype(F32))
            left = lax.broadcasted_iota(jnp.int32, (1, HEAD), 1) < SPAN
            for g in range(groups):
                pair = []
                for b in (2 * g, min(2 * g + 1, blocks - 1)):
                    two = landing[c * blocks + b, SPAN:].astype(F32)
                    pair.append(two[:1] + two[1:2])
                current[g : g + 1] = jnp.where(left, pair[0], pair[1])

        @pl.when(i >= chunks)
        def _():
            current[...] = finish(i - chunks)

        wide = spread(lax.rsqrt(current[...] * (1.0 / width) + EPSILON))
        squared = wide * wide
        x = states[s, whole].astype(F32)
        rq = lax.rsqrt(squared * raw[c, 3] + EPSILON)
        rk = lax.rsqrt(squared * raw[c, 4] + EPSILON)
        qn = (raw[c, 0] * (wide * rq)).astype(BF16)
        kn = (raw[c, 1] * (wide * rk)).astype(BF16)
        v = (raw[c, 2] * wide).astype(BF16)
        near_k = jnp.concatenate([keys[s, span_of(base, SPAN)], kn], axis=0)
        near_v = jnp.concatenate([values[s, span_of(base, SPAN)], v], axis=0)
        scores = [dot_nt(cut(qn, b), cut(near_k, b, 2 * SPAN)) for b in range(blocks)]
        raised = [
            (jnp.exp2(scores[b] * (LOG2E * HEAD**-0.5)) * mask[c * blocks + b]).astype(BF16)
            for b in range(blocks)
        ]
        both = [
            dot(raised[b], jnp.concatenate([cut(near_v, b, 2 * SPAN), ones], axis=1))
            for b in range(blocks)
        ]
        inverse = [1.0 / both[b][:, HEAD:] for b in range(blocks)]
        o = jnp.concatenate([(both[b][:, :HEAD] * inverse[b]).astype(BF16) for b in range(blocks)], axis=0)
        branch = dot(o, weights[s, 3]).astype(BF16)
        new = (x + branch.astype(F32)).astype(BF16)
        wide_new = new.astype(F32)
        states[s + 1, whole] = new
        scale_x[s, whole] = wide
        queries[s, whole] = qn
        keys[s, padded] = kn
        values[s, padded] = v
        mixed[s, whole] = o

        @pl.when(s < SECTIONS - 1)
        def _():
            start(i, packed((wide_new * wide_new).astype(BF16)))
            project(s + 1, c, wide_new)

        scale_q[s, whole] = rq * HEAD**-0.5
        scale_k[s, whole] = rk * HEAD**-0.5
        for b in range(blocks):
            chances[s, c * blocks + b] = (raised[b].astype(F32) * inverse[b]).astype(BF16)
        normed[s, whole] = (x * wide * gain_of(s)).astype(BF16)
        return 0

    lax.fori_loop(0, SECTIONS * chunks, forward, 0)


    def backward(j, _):
        s, c = SECTIONS - 1 - j // chunks, chunks - 1 - j % chunks
        base = c * chunk
        whole = span_of(base, chunk)

        @pl.when(j < chunks)
        def _():
            cot[whole] = states[SECTIONS, whole] * valid[whole]

        @pl.when(j >= chunks)
        def _():
            along = spread(finish(later + j - chunks) * (1.0 / width))
            wide = scale_x[s + 1, whole]
            unit = states[s + 1, whole].astype(F32) * (wide * wide)
            cot[whole] = (base_cot[whole] - unit * along).astype(BF16)

        @pl.when(c == chunks - 1)
        def _():
            carry[...] = jnp.zeros_like(carry)

        g = cot[whole]
        o = mixed[s, whole]
        gm = dot(g, weights_back[s, 3 * HEAD :]).astype(BF16)
        delta = dot((gm.astype(F32) * o.astype(F32)).astype(BF16), ones)
        near = span_of(base, chunk + SPAN)
        near_k, near_v = keys[s, near], values[s, near]
        qn = queries[s, whole]
        share = [chances[s, c * blocks + b] for b in range(blocks)]
        unit_v = [dot_tn(share[b], cut(gm, b)) for b in range(blocks)]
        late_v = [unit_v[b][:SPAN] for b in range(1, blocks)] + [carry[1]]
        carry[1] = unit_v[0][:SPAN]
        all_v = jnp.concatenate([unit_v[b][SPAN:] + late_v[b] for b in range(blocks)], axis=0)
        dv = all_v.astype(BF16)
        xn = normed[s, whole]

        grad_share = [dot_nt(cut(gm, b), cut(near_v, b, 2 * SPAN)) for b in range(blocks)]
        grad_score = [
            (share[b].astype(F32) * (grad_share[b] - cut(delta, b))).astype(BF16) for b in range(blocks)
        ]
        unit_q = [dot(grad_score[b], cut(near_k, b, 2 * SPAN)) for b in range(blocks)]
        unit_k = [dot_tn(grad_score[b], cut(qn, b)) for b in range(blocks)]
        late_k = [unit_k[b][:SPAN] for b in range(1, blocks)] + [carry[0]]
        all_k = jnp.concatenate([unit_k[b][SPAN:] + late_k[b] for b in range(blocks)], axis=0)
        carry[0] = unit_k[0][:SPAN]
        all_q = jnp.concatenate(unit_q, axis=0)
        wide_q = qn.astype(F32)
        wide_k = near_k[SPAN:].astype(F32)
        terms_q = all_q * wide_q
        terms_k = all_k * wide_k
        sq, sk = scale_q[s, whole], scale_k[s, whole]

        @pl.when(s > 0)
        def _():
            small = (EPSILON * HEAD**0.5) * (sq * sq * terms_q + sk * sk * terms_k)
            start(later + j, packed((all_v * near_v[SPAN:].astype(F32) + small).astype(BF16)))

        along_q = dot(terms_q.astype(BF16), mean)
        along_k = dot(terms_k.astype(BF16), mean)
        dq = (sq * (all_q - wide_q * along_q)).astype(BF16)
        dk = (sk * (all_k - wide_k * along_k)).astype(BF16)
        joined = jnp.concatenate([dq, dk, dv], axis=1)

        @pl.when(s > 0)
        def _():
            grad = dot(joined, weights_back[s, : 3 * HEAD]).astype(BF16)
            base_cot[whole] = g.astype(F32) + scale_x[s, whole] * (grad.astype(F32) * gain_of(s))

        both = dot_tn(xn, joined[:, : 2 * HEAD])
        sums[s, 0] += both[:, :HEAD]
        sums[s, 1] += both[:, HEAD:]

        @pl.when(s >= 0)
        def _():
            sums[s, 2] += dot_tn(normed[s, whole], all_v.astype(BF16))
            sums[s, 3] += dot_tn(mixed[s, whole], cot[whole])

        @pl.when(c == 0)
        def _():
            start_halves(s)

        @pl.when((j >= chunks) & (j % chunks == 0))
        def _():
            start_chips(s + 1)

        return 0

    lax.fori_loop(0, SECTIONS * chunks, backward, 0)

    start_chips(0)
    own_sum()


def local(inputs, weights, gains, doc_lengths):
    seq, pipe, dp = lax.axis_size("seq"), lax.axis_size("pipe"), lax.axis_size("dp")
    total = inputs.shape[2] * seq
    width = gains.shape[1]
    rows = total // 2 + 2 * SPAN
    chunks = 2
    chunk = rows // chunks
    across = 4 if seq > 4 else 2
    down = seq // across
    items = 2 * (SECTIONS - 1) * chunks
    groups = -(-chunk // GROUP)
    cfg = dict(
        total=total,
        seq=seq,
        pipe=pipe,
        dp=dp,
        width=width,
        across=across,
        rows=rows,
        chunk=chunk,
        chunks=chunks,
    )
    scratch = [
        pltpu.VMEM((SECTIONS, 4, HEAD, HEAD), BF16),
        pltpu.VMEM((SECTIONS, HEAD), F32),
        pltpu.VMEM(doc_lengths.shape[1:], jnp.int32),
        pltpu.VMEM((SECTIONS, HEAD, 3 * HEAD), BF16),
        pltpu.VMEM((SECTIONS, 4 * HEAD, HEAD), BF16),
        pltpu.VMEM((SECTIONS + 1, rows, HEAD), BF16),
        pltpu.VMEM((SECTIONS, rows, HEAD), BF16),
        pltpu.VMEM((SECTIONS, rows, HEAD), BF16),
        pltpu.VMEM((SECTIONS, SPAN + rows, HEAD), BF16),
        pltpu.VMEM((SECTIONS, SPAN + rows, HEAD), BF16),
        pltpu.VMEM((SECTIONS, rows, HEAD), BF16),
        pltpu.VMEM((SECTIONS, rows // SPAN, SPAN, 2 * SPAN), BF16),
        pltpu.VMEM((SECTIONS, rows, HEAD), F32),
        pltpu.VMEM((SECTIONS, rows, HEAD), F32),
        pltpu.VMEM((SECTIONS, rows, HEAD), F32),
        pltpu.VMEM((rows // SPAN, SPAN, 2 * SPAN), F32),
        pltpu.VMEM((rows, HEAD), BF16),
        pltpu.VMEM((rows, HEAD), BF16),
        pltpu.VMEM((rows, HEAD), F32),
        pltpu.VMEM((2, SPAN, HEAD), F32),
        pltpu.VMEM((SECTIONS, 4, HEAD, HEAD), F32),
        pltpu.VMEM((SECTIONS, 8, HEAD), F32),
        pltpu.VMEM((SPAN + EXTRA, width), BF16),
        pltpu.VMEM((rows // SPAN, SPAN + EXTRA, HEAD), BF16),
        pltpu.VMEM((chunks, 5, chunk, HEAD), F32),
        pltpu.VMEM((8, HEAD), F32),
        pltpu.VMEM((items, groups, HEAD), F32),
        pltpu.VMEM((items, seq - 1, groups, HEAD), F32),
        pltpu.VMEM((SECTIONS, 2, HEAD, HEAD), BF16),
        pltpu.VMEM((SECTIONS, 2, HEAD, HEAD), BF16),
        pltpu.VMEM((SECTIONS, 2, HEAD, HEAD), BF16),
        pltpu.VMEM((2 * dp, HEAD, HEAD), BF16),
        pltpu.VMEM((HEAD, HEAD), BF16),
        pltpu.VMEM((dp - 1, HEAD, HEAD), BF16),
        pltpu.SemaphoreType.DMA((4,)),
        pltpu.SemaphoreType.DMA,
        pltpu.SemaphoreType.DMA((chunks,)),
        pltpu.SemaphoreType.DMA((items,)),
        pltpu.SemaphoreType.DMA((items,)),
        pltpu.SemaphoreType.DMA((SECTIONS,)),
        pltpu.SemaphoreType.DMA((SECTIONS,)),
        pltpu.SemaphoreType.DMA((SECTIONS,)),
        pltpu.SemaphoreType.DMA,
        pltpu.SemaphoreType.DMA,
        pltpu.SemaphoreType.DMA,
    ]
    hbm = pl.BlockSpec(memory_space=pltpu.HBM)
    return pl.pallas_call(
        functools.partial(kernel, cfg),
        out_shape=jax.ShapeDtypeStruct((1, 1, 4, HEAD, HEAD), BF16),
        in_specs=[hbm, hbm, hbm, hbm],
        out_specs=pl.BlockSpec(memory_space=pltpu.VMEM),
        scratch_shapes=scratch,
        compiler_params=pltpu.CompilerParams(
            collective_id=0, has_side_effects=True, vmem_limit_bytes=60 * 1024 * 1024
        ),
    )(inputs, weights, gains, doc_lengths).astype(F32)


def solution(mesh):
    placed = (
        P("dp", None, "seq", None),
        P(None, "seq", None, None, None),
        P(),
        P("dp", None, None),
    )
    return jax.shard_map(
        local,
        mesh=mesh,
        in_specs=placed,
        out_specs=P("pipe", "seq", None, None, None),
        check_vma=False,
    )
```

```python
import functools

import jax
import jax.numpy as jnp
from jax import lax
from jax.experimental import pallas as pl
from jax.experimental.pallas import tpu as pltpu
from jax.sharding import PartitionSpec as P

EPSILON = 1e-06
EXTRA = 16
SECTIONS = 4
SPAN = 64
HEAD = 128
GROUP = 128
F32 = jnp.float32
BF16 = jnp.bfloat16
LOG2E = 1.4426950408889634


def dot(a, b):
    return lax.dot_general(a, b, (((1,), (0,)), ((), ())), preferred_element_type=F32)


def dot_nt(a, b):
    return lax.dot_general(a, b, (((1,), (1,)), ((), ())), preferred_element_type=F32)


def dot_tn(a, b):
    return lax.dot_general(a, b, (((0,), (0,)), ((), ())), preferred_element_type=F32)


def kernel(
    cfg,
    inputs_ref,
    weights_ref,
    gains_ref,
    docs_ref,
    grads_ref,
    weights,
    gains,
    docs,
    weights_in,
    weights_back,
    states,
    normed,
    queries,
    keys,
    values,
    mixed,
    chances,
    scale_q,
    scale_k,
    scale_x,
    mask,
    valid,
    cot,
    base_cot,
    carry,
    sums,
    gain_rows,
    tokens,
    landing,
    raw,
    current,
    sent,
    received,
    half_send,
    half_recv,
    chip_send,
    chip_recv,
    own_send,
    own_recv,
    load_sem,
    in_send,
    in_recv,
    sent_sem,
    received_sem,
    half_send_sem,
    half_recv_sem,
    chip_send_sem,
    chip_recv_sem,
    own_send_sem,
    own_recv_sem,
):
    total, seq, width, across = cfg["total"], cfg["seq"], cfg["width"], cfg["across"]
    rows, chunk, chunks = cfg["rows"], cfg["chunk"], cfg["chunks"]
    pipe, dp = cfg["pipe"], cfg["dp"]
    down = seq // across
    groups, blocks = -(-chunk // GROUP), chunk // SPAN
    all_blocks = rows // SPAN
    place, me, replica = lax.axis_index("pipe"), lax.axis_index("seq"), lax.axis_index("dp")
    micro, half = place >> 1, place & 1
    core = half
    chip = micro * dp + replica
    first_block = half * (seq - all_blocks)
    window = first_block * SPAN
    my_x, my_y = me & (across - 1), me >> (across.bit_length() - 1)
    offsets = [(x, y) for y in range(down) for x in range(across)][1:]
    offsets.sort(key=lambda o: -(min(o[0], across - o[0]) + min(o[1], down - o[1])))

    def peer_at(offset):
        return ((my_y + offset[1]) & (down - 1)) * across + ((my_x + offset[0]) & (across - 1))

    loads = [
        pltpu.make_async_copy(weights_ref.at[:, 0], weights, load_sem.at[0]),
        pltpu.make_async_copy(
            gains_ref.at[:, pl.ds(pl.multiple_of(me * HEAD, HEAD), HEAD)], gains, load_sem.at[1]
        ),
        pltpu.make_async_copy(docs_ref.at[0], docs, load_sem.at[2]),
        pltpu.make_async_copy(inputs_ref.at[0, micro], tokens.at[pl.ds(0, SPAN)], load_sem.at[3]),
    ]
    for load in loads:
        load.start()

    barrier = pltpu.get_barrier_semaphore()

    distant = [o for o in offsets if min(o[0], across - o[0]) + min(o[1], down - o[1]) > 3]
    close = offsets[len(distant) :]
    for offset in distant:
        pl.semaphore_signal(barrier, inc=1, device_id={"seq": peer_at(offset)})
    for q in range(pipe):
        for r in range(dp):
            if q or r:
                there = {"pipe": place ^ q, "dp": replica ^ r}
                pl.semaphore_signal(barrier, inc=1, device_id=there)
    for offset in close:
        pl.semaphore_signal(barrier, inc=1, device_id={"seq": peer_at(offset)})

    slot = me - first_block
    own_blocks = seq // 2
    lead = all_blocks - own_blocks
    in_window = (slot >= half * lead) & (slot < own_blocks + 1 + half * (all_blocks - own_blocks - 1))
    part = jnp.where(slot >= blocks, 1, 0)

    def piece(head):
        return tokens.at[:, pl.ds(pl.multiple_of(head * HEAD, HEAD), HEAD)]

    later = (SECTIONS - 1) * chunks
    ones = jnp.full((HEAD, HEAD), 1.0, BF16)
    mean = jnp.full((HEAD, HEAD), 1.0 / HEAD, BF16)
    row8 = lax.broadcasted_iota(jnp.int32, (8, HEAD), 0)
    row16 = lax.broadcasted_iota(jnp.int32, (16, groups * HEAD), 0) % 8
    lane16 = lax.broadcasted_iota(jnp.int32, (16, groups * HEAD), 1) // HEAD
    selector = jnp.where(row16 == lane16, 1.0, 0.0).astype(BF16)

    for load in loads:
        load.wait()

    both = docs[...].astype(F32)
    lengths = jnp.where(micro == 0, both[0:1], both[1:2]).astype(BF16)
    count = lengths.shape[1]
    earlier = lax.broadcasted_iota(jnp.int32, (count, HEAD), 0) < lax.broadcasted_iota(
        jnp.int32, (count, HEAD), 1
    )
    starts = dot(jnp.broadcast_to(lengths, (8, count)), jnp.where(earlier, 1.0, 0.0).astype(BF16))[:1]
    mid = total // 2

    def prepare():
        def make_mask(b, _):
            base = window + b * SPAN
            token = base + lax.broadcasted_iota(jnp.int32, (SPAN, HEAD), 0)
            key = base - SPAN + lax.broadcasted_iota(jnp.int32, (SPAN, HEAD), 1)
            reach = jnp.where(starts <= token.astype(F32), starts, 0.0)
            begin = jnp.max(reach, axis=1, keepdims=True)
            allowed = (key.astype(F32) >= begin) & (key <= token)
            mask[b] = jnp.where(allowed, 1.0, 0.0)
            late = jnp.where(begin >= mid, 1.0, 0.0)
            mine = jnp.where(half == 1, late, 1.0 - late)
            valid[pl.ds(pl.multiple_of(b * SPAN, SPAN), SPAN)] = jnp.broadcast_to(mine, (SPAN, HEAD)).astype(BF16)
            return 0

        lax.fori_loop(0, all_blocks, make_mask, 0)
        for s in range(SECTIONS):
            keys[s, :SPAN] = jnp.zeros((SPAN, HEAD), BF16)
            values[s, :SPAN] = jnp.zeros((SPAN, HEAD), BF16)
            gain_rows[s] = jnp.broadcast_to(gains[s : s + 1], (8, HEAD))
        sums[...] = jnp.zeros_like(sums)

        @pl.when(half == 0)
        def _():
            landing[own_blocks + 1 :] = jnp.zeros((all_blocks - own_blocks - 1, SPAN + EXTRA, HEAD), BF16)

        @pl.when(half == 1)
        def _():
            landing[:lead] = jnp.zeros((lead, SPAN + EXTRA, HEAD), BF16)

        current[...] = jnp.zeros_like(current)

        def arrange(s, _):
            for m in range(4):
                block = weights[s, m]
                if m < 3:
                    weights_in[s, :, m * HEAD : (m + 1) * HEAD] = block
                weights_back[s, m * HEAD : (m + 1) * HEAD] = jnp.transpose(block.astype(F32)).astype(BF16)
            return 0

        lax.fori_loop(0, SECTIONS, arrange, 0)

    squares = jnp.zeros((SPAN, HEAD), F32)
    for h in range(seq):
        feature = tokens[:SPAN, h * HEAD : (h + 1) * HEAD].astype(F32)
        squares = squares + feature * feature
    twice = jnp.concatenate([squares, squares], axis=0)
    high = twice.astype(BF16)
    low = (twice - high.astype(F32)).astype(BF16)
    sum_row = (dot_nt(ones[:8], high) + dot_nt(ones[:8], low))[:1]
    high = sum_row.astype(BF16)
    low = (sum_row - high.astype(F32)).astype(BF16)
    extra = jnp.concatenate([high, low, jnp.zeros((EXTRA - 2, HEAD), BF16)], axis=0)
    for h in range(seq):
        tokens[SPAN:, h * HEAD : (h + 1) * HEAD] = extra

    early = (part == 0) & in_window

    @pl.when(early)
    def _():
        prepare()

    pl.semaphore_wait(barrier, seq - 1 + pipe * dp - 1)

    @pl.when(jnp.logical_not(early))
    def _():
        prepare()

    @pl.when(in_window)
    def _():
        for offset in offsets:
            peer = peer_at(offset)
            pltpu.make_async_remote_copy(
                src_ref=piece(peer),
                dst_ref=landing.at[slot],
                send_sem=in_send,
                recv_sem=in_recv.at[part],
                device_id={"seq": peer},
            ).start()
        pltpu.make_async_copy(piece(me), landing.at[slot], in_recv.at[part]).start()

    def packed(term):
        if groups * GROUP > chunk:
            spare = jnp.zeros((groups * GROUP - chunk, HEAD), BF16)
            term = jnp.concatenate([term, spare], axis=0)
        total_rows = None
        for g in range(groups):
            pick = jnp.where(row8 == g, 1.0, 0.0).astype(BF16)
            part = dot_nt(pick, term[g * GROUP : (g + 1) * GROUP])
            total_rows = part if total_rows is None else total_rows + part
        return total_rows

    def spread(packed_rows):
        high = packed_rows.astype(BF16)
        low = (packed_rows - high.astype(F32)).astype(BF16)
        wide = dot_tn(jnp.concatenate([high, low], axis=0), selector)
        parts = [wide[:, g * HEAD : (g + 1) * HEAD] for g in range(groups)]
        return jnp.concatenate(parts, axis=0)[:chunk]

    def start(item, part):
        sent[item] = part[:groups]
        for n, offset in enumerate(offsets):
            pltpu.make_async_remote_copy(
                src_ref=sent.at[item],
                dst_ref=received.at[item, n],
                send_sem=sent_sem.at[item],
                recv_sem=received_sem.at[item],
                device_id={"seq": peer_at(offset)},
            ).start()

    def finish(item):
        pltpu.make_async_copy(received.at[item], received.at[item], received_sem.at[item]).wait()
        parts = [sent[item]] + [received[item, n] for n in range(seq - 1)]
        while len(parts) > 1:
            parts = [a + b for a, b in zip(parts[::2], parts[1::2])]
        spare = jnp.zeros((8 - groups, HEAD), F32)
        return jnp.concatenate([parts[0], spare], axis=0) if groups < 8 else parts[0]

    def span_of(start, size):
        return pl.ds(pl.multiple_of(start, SPAN), size)

    def gain_of(s):
        return gain_rows[s][:1]

    def cut(value, b, size=SPAN):
        return value[b * SPAN : b * SPAN + size]

    def half_rows(p):
        return pl.ds(p * SPAN, SPAN)

    def start_halves(s):
        for m in range(2):
            theirs = jnp.where(core == 0, sums[s, 2 + m], sums[s, m])
            half_send[s, m] = theirs.astype(BF16)
        pltpu.make_async_remote_copy(
            src_ref=half_send.at[s],
            dst_ref=half_recv.at[s],
            send_sem=half_send_sem.at[s],
            recv_sem=half_recv_sem.at[s],
            device_id={"pipe": micro * 2 + 1 - core},
        ).start()

    def start_chips(s):
        pltpu.make_async_copy(half_recv.at[s], half_recv.at[s], half_recv_sem.at[s]).wait()
        for m in range(2):
            ours = jnp.where(core == 0, sums[s, m], sums[s, 2 + m])
            chip_send[s, m] = (ours + half_recv[s, m].astype(F32)).astype(BF16)
        for p in range(2):
            for m in range(2):
                owner = core * 2 + m
                here = (place == s) & (replica == owner)
                source, target = chip_send.at[s, m, half_rows(p)], chip_recv.at[chip, half_rows(p)]

                @pl.when(here)
                def _():
                    pltpu.make_async_copy(source, target, chip_recv_sem.at[p]).start()

                @pl.when(jnp.logical_not(here))
                def _():
                    pltpu.make_async_remote_copy(
                        src_ref=source,
                        dst_ref=target,
                        send_sem=chip_send_sem.at[s],
                        recv_sem=chip_recv_sem.at[p],
                        device_id={"pipe": s, "dp": owner},
                    ).start()

    def drain():
        def drain_item(item, _):
            pltpu.make_async_copy(received.at[item], received.at[item], sent_sem.at[item]).wait()
            return 0

        lax.fori_loop(0, 2 * later, drain_item, 0)

        def drain_grads(s, _):
            pltpu.make_async_copy(half_send.at[s], half_send.at[s], half_send_sem.at[s]).wait()
            here = (place == s) & (replica // 2 == core)

            @pl.when(here)
            def _():
                pltpu.make_async_copy(chip_send.at[s, 0], chip_send.at[s, 0], chip_send_sem.at[s]).wait()

            @pl.when(jnp.logical_not(here))
            def _():
                pltpu.make_async_copy(chip_send.at[s], chip_send.at[s], chip_send_sem.at[s]).wait()

            return 0

        lax.fori_loop(0, SECTIONS, drain_grads, 0)

        @pl.when(in_window)
        def _():
            all_sent = tokens.at[:, pl.ds(0, (seq - 1) * HEAD)]
            pltpu.make_async_copy(all_sent, all_sent, in_send).wait()

    def own_sum():
        for p in range(2):
            at = half_rows(p)
            there = chip_recv.at[:, at]
            pltpu.make_async_copy(there, there, chip_recv_sem.at[p]).wait()
            part = chip_recv[0, at].astype(F32)
            for k in range(1, 2 * dp):
                part = part + chip_recv[k, at].astype(F32)
            own_send[at] = part.astype(BF16)
            for o in range(1, dp):
                pltpu.make_async_remote_copy(
                    src_ref=own_send.at[at],
                    dst_ref=own_recv.at[o - 1, at],
                    send_sem=own_send_sem.at[p],
                    recv_sem=own_recv_sem.at[p],
                    device_id={"dp": (replica + o) & (dp - 1)},
                ).start()
        grads_ref[0, 0, replica] = own_send[...]
        drain()
        for p in range(2):
            at = half_rows(p)
            there = own_recv.at[:, at]
            pltpu.make_async_copy(there, there, own_recv_sem.at[p]).wait()
            for o in range(1, dp):
                grads_ref[0, 0, (replica - o) & (dp - 1), at] = own_recv[o - 1, at]
        for p in range(2):
            there = own_recv.at[:, half_rows(p)]
            pltpu.make_async_copy(there, there, own_send_sem.at[p]).wait()

    def project(s, c, x):
        qkv = dot((x * gain_of(s)).astype(BF16), weights_in[s])
        q, k = qkv[:, :HEAD], qkv[:, HEAD : 2 * HEAD]
        raw[c, 0], raw[c, 1], raw[c, 2] = q, k, qkv[:, 2 * HEAD :]
        raw[c, 3] = dot((q * q).astype(BF16), mean)
        raw[c, 4] = dot((k * k).astype(BF16), mean)

    def arrived(c):
        for h in range(2):
            first = max(c * blocks, lead if h else 0)
            last = min((c + 1) * blocks, all_blocks if h else own_blocks + 1)

            @pl.when(half == h)
            def _():
                there = landing.at[pl.ds(first, last - first)]
                pltpu.make_async_copy(there, there, in_recv.at[c]).wait()

    def forward(i, _):
        s, c = i // chunks, i % chunks
        base = c * chunk
        whole = span_of(base, chunk)
        padded = span_of(base + SPAN, chunk)

        for k in range(chunks):
            @pl.when(i == k)
            def _():
                arrived(k)

        @pl.when(i < chunks)
        def _():
            new = jnp.concatenate([landing[c * blocks + b, :SPAN] for b in range(blocks)], axis=0)
            states[0, whole] = new
            project(0, c, new.astype(F32))
            left = lax.broadcasted_iota(jnp.int32, (1, HEAD), 1) < SPAN
            for g in range(groups):
                pair = []
                for b in (2 * g, min(2 * g + 1, blocks - 1)):
                    two = landing[c * blocks + b, SPAN:].astype(F32)
                    pair.append(two[:1] + two[1:2])
                current[g : g + 1] = jnp.where(left, pair[0], pair[1])

        @pl.when(i >= chunks)
        def _():
            current[...] = finish(i - chunks)

        wide = spread(lax.rsqrt(current[...] * (1.0 / width) + EPSILON))
        squared = wide * wide
        x = states[s, whole].astype(F32)
        rq = lax.rsqrt(squared * raw[c, 3] + EPSILON)
        rk = lax.rsqrt(squared * raw[c, 4] + EPSILON)
        qn = (raw[c, 0] * (wide * rq)).astype(BF16)
        kn = (raw[c, 1] * (wide * rk)).astype(BF16)
        v = (raw[c, 2] * wide).astype(BF16)
        near_k = jnp.concatenate([keys[s, span_of(base, SPAN)], kn], axis=0)
        near_v = jnp.concatenate([values[s, span_of(base, SPAN)], v], axis=0)
        scores = [dot_nt(cut(qn, b), cut(near_k, b, 2 * SPAN)) for b in range(blocks)]
        raised = [
            (jnp.exp2(scores[b] * (LOG2E * HEAD**-0.5)) * mask[c * blocks + b]).astype(BF16)
            for b in range(blocks)
        ]
        both = [
            dot(raised[b], jnp.concatenate([cut(near_v, b, 2 * SPAN), ones], axis=1))
            for b in range(blocks)
        ]
        inverse = [1.0 / both[b][:, HEAD:] for b in range(blocks)]
        o = jnp.concatenate([(both[b][:, :HEAD] * inverse[b]).astype(BF16) for b in range(blocks)], axis=0)
        branch = dot(o, weights[s, 3]).astype(BF16)
        new = (x + branch.astype(F32)).astype(BF16)
        wide_new = new.astype(F32)
        states[s + 1, whole] = new
        scale_x[s, whole] = wide
        queries[s, whole] = qn
        keys[s, padded] = kn
        values[s, padded] = v
        mixed[s, whole] = o

        @pl.when(s < SECTIONS - 1)
        def _():
            start(i, packed((wide_new * wide_new).astype(BF16)))
            project(s + 1, c, wide_new)

        scale_q[s, whole] = rq * HEAD**-0.5
        scale_k[s, whole] = rk * HEAD**-0.5
        for b in range(blocks):
            chances[s, c * blocks + b] = (raised[b].astype(F32) * inverse[b]).astype(BF16)
        normed[s, whole] = (x * wide * gain_of(s)).astype(BF16)
        return 0

    lax.fori_loop(0, SECTIONS * chunks, forward, 0)


    def backward(j, _):
        s, c = SECTIONS - 1 - j // chunks, chunks - 1 - j % chunks
        base = c * chunk
        whole = span_of(base, chunk)

        @pl.when(j < chunks)
        def _():
            cot[whole] = states[SECTIONS, whole] * valid[whole]

        @pl.when(j >= chunks)
        def _():
            along = spread(finish(later + j - chunks) * (1.0 / width))
            wide = scale_x[s + 1, whole]
            unit = states[s + 1, whole].astype(F32) * (wide * wide)
            cot[whole] = (base_cot[whole] - unit * along).astype(BF16)

        @pl.when(c == chunks - 1)
        def _():
            carry[...] = jnp.zeros_like(carry)

        g = cot[whole]
        o = mixed[s, whole]
        gm = dot(g, weights_back[s, 3 * HEAD :]).astype(BF16)
        delta = dot((gm.astype(F32) * o.astype(F32)).astype(BF16), ones)
        near = span_of(base, chunk + SPAN)
        near_k, near_v = keys[s, near], values[s, near]
        qn = queries[s, whole]
        share = [chances[s, c * blocks + b] for b in range(blocks)]
        unit_v = [dot_tn(share[b], cut(gm, b)) for b in range(blocks)]
        late_v = [unit_v[b][:SPAN] for b in range(1, blocks)] + [carry[1]]
        carry[1] = unit_v[0][:SPAN]
        all_v = jnp.concatenate([unit_v[b][SPAN:] + late_v[b] for b in range(blocks)], axis=0)
        dv = all_v.astype(BF16)
        xn = normed[s, whole]

        grad_share = [dot_nt(cut(gm, b), cut(near_v, b, 2 * SPAN)) for b in range(blocks)]
        grad_score = [
            (share[b].astype(F32) * (grad_share[b] - cut(delta, b))).astype(BF16) for b in range(blocks)
        ]
        unit_q = [dot(grad_score[b], cut(near_k, b, 2 * SPAN)) for b in range(blocks)]
        unit_k = [dot_tn(grad_score[b], cut(qn, b)) for b in range(blocks)]
        late_k = [unit_k[b][:SPAN] for b in range(1, blocks)] + [carry[0]]
        all_k = jnp.concatenate([unit_k[b][SPAN:] + late_k[b] for b in range(blocks)], axis=0)
        carry[0] = unit_k[0][:SPAN]
        all_q = jnp.concatenate(unit_q, axis=0)
        wide_q = qn.astype(F32)
        wide_k = near_k[SPAN:].astype(F32)
        terms_q = all_q * wide_q
        terms_k = all_k * wide_k
        sq, sk = scale_q[s, whole], scale_k[s, whole]

        @pl.when(s > 0)
        def _():
            small = (EPSILON * HEAD**0.5) * (sq * sq * terms_q + sk * sk * terms_k)
            start(later + j, packed((all_v * near_v[SPAN:].astype(F32) + small).astype(BF16)))

        along_q = dot(terms_q.astype(BF16), mean)
        along_k = dot(terms_k.astype(BF16), mean)
        dq = (sq * (all_q - wide_q * along_q)).astype(BF16)
        dk = (sk * (all_k - wide_k * along_k)).astype(BF16)
        joined = jnp.concatenate([dq, dk, dv], axis=1)

        @pl.when(s > 0)
        def _():
            grad = dot(joined, weights_back[s, : 3 * HEAD]).astype(BF16)
            base_cot[whole] = g.astype(F32) + scale_x[s, whole] * (grad.astype(F32) * gain_of(s))

        both = dot_tn(xn, joined[:, : 2 * HEAD])
        sums[s, 0] += both[:, :HEAD]
        sums[s, 1] += both[:, HEAD:]

        @pl.when(s >= 0)
        def _():
            sums[s, 2] += dot_tn(normed[s, whole], all_v.astype(BF16))
            sums[s, 3] += dot_tn(mixed[s, whole], cot[whole])

        @pl.when(c == 0)
        def _():
            start_halves(s)

        @pl.when((j >= chunks) & (j % chunks == 0))
        def _():
            start_chips(s + 1)

        return 0

    lax.fori_loop(0, SECTIONS * chunks, backward, 0)

    start_chips(0)
    own_sum()


def local(inputs, weights, gains, doc_lengths):
    seq, pipe, dp = lax.axis_size("seq"), lax.axis_size("pipe"), lax.axis_size("dp")
    total = inputs.shape[2] * seq
    width = gains.shape[1]
    rows = total // 2 + 2 * SPAN
    chunks = 2
    chunk = rows // chunks
    across = 4 if seq > 4 else 2
    down = seq // across
    items = 2 * (SECTIONS - 1) * chunks
    groups = -(-chunk // GROUP)
    cfg = dict(
        total=total,
        seq=seq,
        pipe=pipe,
        dp=dp,
        width=width,
        across=across,
        rows=rows,
        chunk=chunk,
        chunks=chunks,
    )
    scratch = [
        pltpu.VMEM((SECTIONS, 4, HEAD, HEAD), BF16),
        pltpu.VMEM((SECTIONS, HEAD), F32),
        pltpu.VMEM(doc_lengths.shape[1:], jnp.int32),
        pltpu.VMEM((SECTIONS, HEAD, 3 * HEAD), BF16),
        pltpu.VMEM((SECTIONS, 4 * HEAD, HEAD), BF16),
        pltpu.VMEM((SECTIONS + 1, rows, HEAD), BF16),
        pltpu.VMEM((SECTIONS, rows, HEAD), BF16),
        pltpu.VMEM((SECTIONS, rows, HEAD), BF16),
        pltpu.VMEM((SECTIONS, SPAN + rows, HEAD), BF16),
        pltpu.VMEM((SECTIONS, SPAN + rows, HEAD), BF16),
        pltpu.VMEM((SECTIONS, rows, HEAD), BF16),
        pltpu.VMEM((SECTIONS, rows // SPAN, SPAN, 2 * SPAN), BF16),
        pltpu.VMEM((SECTIONS, rows, HEAD), F32),
        pltpu.VMEM((SECTIONS, rows, HEAD), F32),
        pltpu.VMEM((SECTIONS, rows, HEAD), F32),
        pltpu.VMEM((rows // SPAN, SPAN, 2 * SPAN), F32),
        pltpu.VMEM((rows, HEAD), BF16),
        pltpu.VMEM((rows, HEAD), BF16),
        pltpu.VMEM((rows, HEAD), F32),
        pltpu.VMEM((2, SPAN, HEAD), F32),
        pltpu.VMEM((SECTIONS, 4, HEAD, HEAD), F32),
        pltpu.VMEM((SECTIONS, 8, HEAD), F32),
        pltpu.VMEM((SPAN + EXTRA, width), BF16),
        pltpu.VMEM((rows // SPAN, SPAN + EXTRA, HEAD), BF16),
        pltpu.VMEM((chunks, 5, chunk, HEAD), F32),
        pltpu.VMEM((8, HEAD), F32),
        pltpu.VMEM((items, groups, HEAD), F32),
        pltpu.VMEM((items, seq - 1, groups, HEAD), F32),
        pltpu.VMEM((SECTIONS, 2, HEAD, HEAD), BF16),
        pltpu.VMEM((SECTIONS, 2, HEAD, HEAD), BF16),
        pltpu.VMEM((SECTIONS, 2, HEAD, HEAD), BF16),
        pltpu.VMEM((2 * dp, HEAD, HEAD), BF16),
        pltpu.VMEM((HEAD, HEAD), BF16),
        pltpu.VMEM((dp - 1, HEAD, HEAD), BF16),
        pltpu.SemaphoreType.DMA((4,)),
        pltpu.SemaphoreType.DMA,
        pltpu.SemaphoreType.DMA((chunks,)),
        pltpu.SemaphoreType.DMA((items,)),
        pltpu.SemaphoreType.DMA((items,)),
        pltpu.SemaphoreType.DMA((SECTIONS,)),
        pltpu.SemaphoreType.DMA((SECTIONS,)),
        pltpu.SemaphoreType.DMA((SECTIONS,)),
        pltpu.SemaphoreType.DMA((2,)),
        pltpu.SemaphoreType.DMA((2,)),
        pltpu.SemaphoreType.DMA((2,)),
    ]
    hbm = pl.BlockSpec(memory_space=pltpu.HBM)
    return pl.pallas_call(
        functools.partial(kernel, cfg),
        out_shape=jax.ShapeDtypeStruct((1, 1, 4, HEAD, HEAD), BF16),
        in_specs=[hbm, hbm, hbm, hbm],
        out_specs=pl.BlockSpec(memory_space=pltpu.VMEM),
        scratch_shapes=scratch,
        compiler_params=pltpu.CompilerParams(
            collective_id=0, has_side_effects=True, vmem_limit_bytes=60 * 1024 * 1024
        ),
    )(inputs, weights, gains, doc_lengths).astype(F32)


def solution(mesh):
    placed = (
        P("dp", None, "seq", None),
        P(None, "seq", None, None, None),
        P(),
        P("dp", None, None),
    )
    return jax.shard_map(
        local,
        mesh=mesh,
        in_specs=placed,
        out_specs=P("pipe", "seq", None, None, None),
        check_vma=False,
    )
```

```python
import functools

import jax
import jax.numpy as jnp
from jax import lax
from jax.experimental import pallas as pl
from jax.experimental.pallas import tpu as pltpu
from jax.sharding import PartitionSpec as P

EPSILON = 1e-06
EXTRA = 16
SECTIONS = 4
SPAN = 64
HEAD = 128
GROUP = 128
F32 = jnp.float32
BF16 = jnp.bfloat16
LOG2E = 1.4426950408889634


def dot(a, b):
    return lax.dot_general(a, b, (((1,), (0,)), ((), ())), preferred_element_type=F32)


def dot_nt(a, b):
    return lax.dot_general(a, b, (((1,), (1,)), ((), ())), preferred_element_type=F32)


def dot_tn(a, b):
    return lax.dot_general(a, b, (((0,), (0,)), ((), ())), preferred_element_type=F32)


def kernel(
    cfg,
    inputs_ref,
    weights_ref,
    gains_ref,
    docs_ref,
    grads_ref,
    weights,
    gains,
    docs,
    weights_in,
    weights_back,
    states,
    normed,
    queries,
    keys,
    values,
    mixed,
    chances,
    scale_q,
    scale_k,
    scale_x,
    mask,
    valid,
    cot,
    base_cot,
    carry,
    sums,
    gain_rows,
    tokens,
    landing,
    raw,
    current,
    sent,
    received,
    half_send,
    half_recv,
    chip_send,
    chip_recv,
    own_send,
    own_recv,
    load_sem,
    in_send,
    in_recv,
    sent_sem,
    received_sem,
    half_send_sem,
    half_recv_sem,
    chip_send_sem,
    chip_recv_sem,
    own_send_sem,
    own_recv_sem,
):
    total, seq, width, across = cfg["total"], cfg["seq"], cfg["width"], cfg["across"]
    rows, chunk, chunks = cfg["rows"], cfg["chunk"], cfg["chunks"]
    pipe, dp = cfg["pipe"], cfg["dp"]
    down = seq // across
    groups, blocks = -(-chunk // GROUP), chunk // SPAN
    all_blocks = rows // SPAN
    place, me, replica = lax.axis_index("pipe"), lax.axis_index("seq"), lax.axis_index("dp")
    micro, half = place >> 1, place & 1
    core = half
    chip = micro * dp + replica
    first_block = half * (seq - all_blocks)
    window = first_block * SPAN
    my_x, my_y = me & (across - 1), me >> (across.bit_length() - 1)
    offsets = [(x, y) for y in range(down) for x in range(across)][1:]
    offsets.sort(key=lambda o: -(min(o[0], across - o[0]) + min(o[1], down - o[1])))

    def peer_at(offset):
        return ((my_y + offset[1]) & (down - 1)) * across + ((my_x + offset[0]) & (across - 1))

    loads = [
        pltpu.make_async_copy(weights_ref.at[:, 0], weights, load_sem.at[0]),
        pltpu.make_async_copy(
            gains_ref.at[:, pl.ds(pl.multiple_of(me * HEAD, HEAD), HEAD)], gains, load_sem.at[1]
        ),
        pltpu.make_async_copy(docs_ref.at[0], docs, load_sem.at[2]),
        pltpu.make_async_copy(inputs_ref.at[0, micro], tokens.at[pl.ds(0, SPAN)], load_sem.at[3]),
    ]
    for load in loads:
        load.start()

    barrier = pltpu.get_barrier_semaphore()

    distant = [o for o in offsets if min(o[0], across - o[0]) + min(o[1], down - o[1]) > 3]
    close = offsets[len(distant) :]
    for offset in distant:
        pl.semaphore_signal(barrier, inc=1, device_id={"seq": peer_at(offset)})
    for q in range(pipe):
        for r in range(dp):
            if q or r:
                there = {"pipe": place ^ q, "dp": replica ^ r}
                pl.semaphore_signal(barrier, inc=1, device_id=there)
    for offset in close:
        pl.semaphore_signal(barrier, inc=1, device_id={"seq": peer_at(offset)})

    slot = me - first_block
    own_blocks = seq // 2
    lead = all_blocks - own_blocks
    in_window = (slot >= half * lead) & (slot < own_blocks + 1 + half * (all_blocks - own_blocks - 1))
    part = jnp.where(slot >= blocks, 1, 0)

    def piece(head):
        return tokens.at[:, pl.ds(pl.multiple_of(head * HEAD, HEAD), HEAD)]

    later = (SECTIONS - 1) * chunks
    ones = jnp.full((HEAD, HEAD), 1.0, BF16)
    mean = jnp.full((HEAD, HEAD), 1.0 / HEAD, BF16)
    row8 = lax.broadcasted_iota(jnp.int32, (8, HEAD), 0)
    row16 = lax.broadcasted_iota(jnp.int32, (16, groups * HEAD), 0) % 8
    lane16 = lax.broadcasted_iota(jnp.int32, (16, groups * HEAD), 1) // HEAD
    selector = jnp.where(row16 == lane16, 1.0, 0.0).astype(BF16)

    for load in loads:
        load.wait()

    both = docs[...].astype(F32)
    lengths = jnp.where(micro == 0, both[0:1], both[1:2]).astype(BF16)
    count = lengths.shape[1]
    earlier = lax.broadcasted_iota(jnp.int32, (count, HEAD), 0) < lax.broadcasted_iota(
        jnp.int32, (count, HEAD), 1
    )
    starts = dot(jnp.broadcast_to(lengths, (8, count)), jnp.where(earlier, 1.0, 0.0).astype(BF16))[:1]
    mid = total // 2

    def prepare():
        def make_mask(b, _):
            base = window + b * SPAN
            token = base + lax.broadcasted_iota(jnp.int32, (SPAN, HEAD), 0)
            key = base - SPAN + lax.broadcasted_iota(jnp.int32, (SPAN, HEAD), 1)
            reach = jnp.where(starts <= token.astype(F32), starts, 0.0)
            begin = jnp.max(reach, axis=1, keepdims=True)
            allowed = (key.astype(F32) >= begin) & (key <= token)
            mask[b] = jnp.where(allowed, 1.0, 0.0).astype(BF16)
            late = jnp.where(begin >= mid, 1.0, 0.0)
            mine = jnp.where(half == 1, late, 1.0 - late)
            valid[pl.ds(pl.multiple_of(b * SPAN, SPAN), SPAN)] = jnp.broadcast_to(mine, (SPAN, HEAD)).astype(BF16)
            return 0

        lax.fori_loop(0, all_blocks, make_mask, 0)
        for s in range(SECTIONS):
            keys[s, :SPAN] = jnp.zeros((SPAN, HEAD), BF16)
            values[s, :SPAN] = jnp.zeros((SPAN, HEAD), BF16)
            gain_rows[s] = jnp.broadcast_to(gains[s : s + 1], (8, HEAD))
        sums[...] = jnp.zeros_like(sums)

        @pl.when(half == 0)
        def _():
            landing[own_blocks + 1 :] = jnp.zeros((all_blocks - own_blocks - 1, SPAN + EXTRA, HEAD), BF16)

        @pl.when(half == 1)
        def _():
            landing[:lead] = jnp.zeros((lead, SPAN + EXTRA, HEAD), BF16)

        current[...] = jnp.zeros_like(current)

        def arrange(s, _):
            for m in range(4):
                block = weights[s, m]
                if m < 3:
                    weights_in[s, :, m * HEAD : (m + 1) * HEAD] = block
                weights_back[s, m * HEAD : (m + 1) * HEAD] = jnp.transpose(block.astype(F32)).astype(BF16)
            return 0

        lax.fori_loop(0, SECTIONS, arrange, 0)

    squares = jnp.zeros((SPAN, HEAD), F32)
    for h in range(seq):
        feature = tokens[:SPAN, h * HEAD : (h + 1) * HEAD].astype(F32)
        squares = squares + feature * feature
    twice = jnp.concatenate([squares, squares], axis=0)
    high = twice.astype(BF16)
    low = (twice - high.astype(F32)).astype(BF16)
    sum_row = (dot_nt(ones[:8], high) + dot_nt(ones[:8], low))[:1]
    high = sum_row.astype(BF16)
    low = (sum_row - high.astype(F32)).astype(BF16)
    extra = jnp.concatenate([high, low, jnp.zeros((EXTRA - 2, HEAD), BF16)], axis=0)
    for h in range(seq):
        tokens[SPAN:, h * HEAD : (h + 1) * HEAD] = extra

    early = (part == 0) & in_window

    @pl.when(early)
    def _():
        prepare()

    pl.semaphore_wait(barrier, seq - 1 + pipe * dp - 1)

    @pl.when(jnp.logical_not(early))
    def _():
        prepare()

    @pl.when(in_window)
    def _():
        for offset in offsets:
            peer = peer_at(offset)
            pltpu.make_async_remote_copy(
                src_ref=piece(peer),
                dst_ref=landing.at[slot],
                send_sem=in_send,
                recv_sem=in_recv.at[part],
                device_id={"seq": peer},
            ).start()
        pltpu.make_async_copy(piece(me), landing.at[slot], in_recv.at[part]).start()

    def packed(term):
        if groups * GROUP > chunk:
            spare = jnp.zeros((groups * GROUP - chunk, HEAD), BF16)
            term = jnp.concatenate([term, spare], axis=0)
        total_rows = None
        for g in range(groups):
            pick = jnp.where(row8 == g, 1.0, 0.0).astype(BF16)
            part = dot_nt(pick, term[g * GROUP : (g + 1) * GROUP])
            total_rows = part if total_rows is None else total_rows + part
        return total_rows

    def spread(packed_rows):
        high = packed_rows.astype(BF16)
        low = (packed_rows - high.astype(F32)).astype(BF16)
        wide = dot_tn(jnp.concatenate([high, low], axis=0), selector)
        parts = [wide[:, g * HEAD : (g + 1) * HEAD] for g in range(groups)]
        return jnp.concatenate(parts, axis=0)[:chunk]

    def start(item, part):
        sent[item] = part[:groups]
        for n, offset in enumerate(offsets):
            pltpu.make_async_remote_copy(
                src_ref=sent.at[item],
                dst_ref=received.at[item, n],
                send_sem=sent_sem.at[item],
                recv_sem=received_sem.at[item],
                device_id={"seq": peer_at(offset)},
            ).start()

    def finish(item):
        pltpu.make_async_copy(received.at[item], received.at[item], received_sem.at[item]).wait()
        parts = [sent[item]] + [received[item, n] for n in range(seq - 1)]
        while len(parts) > 1:
            parts = [a + b for a, b in zip(parts[::2], parts[1::2])]
        spare = jnp.zeros((8 - groups, HEAD), F32)
        return jnp.concatenate([parts[0], spare], axis=0) if groups < 8 else parts[0]

    def span_of(start, size):
        return pl.ds(pl.multiple_of(start, SPAN), size)

    def gain_of(s):
        return gain_rows[s][:1]

    def cut(value, b, size=SPAN):
        return value[b * SPAN : b * SPAN + size]

    def half_rows(p):
        return pl.ds(p * SPAN, SPAN)

    def start_halves(s):
        for m in range(2):
            theirs = jnp.where(core == 0, sums[s, 2 + m], sums[s, m])
            half_send[s, m] = theirs.astype(BF16)
        pltpu.make_async_remote_copy(
            src_ref=half_send.at[s],
            dst_ref=half_recv.at[s],
            send_sem=half_send_sem.at[s],
            recv_sem=half_recv_sem.at[s],
            device_id={"pipe": micro * 2 + 1 - core},
        ).start()

    def start_chips(s):
        pltpu.make_async_copy(half_recv.at[s], half_recv.at[s], half_recv_sem.at[s]).wait()
        for m in range(2):
            ours = jnp.where(core == 0, sums[s, m], sums[s, 2 + m])
            chip_send[s, m] = (ours + half_recv[s, m].astype(F32)).astype(BF16)
        for p in range(2):
            for m in range(2):
                owner = core * 2 + m
                here = (place == s) & (replica == owner)
                source, target = chip_send.at[s, m, half_rows(p)], chip_recv.at[chip, half_rows(p)]

                @pl.when(here)
                def _():
                    pltpu.make_async_copy(source, target, chip_recv_sem.at[p]).start()

                @pl.when(jnp.logical_not(here))
                def _():
                    pltpu.make_async_remote_copy(
                        src_ref=source,
                        dst_ref=target,
                        send_sem=chip_send_sem.at[s],
                        recv_sem=chip_recv_sem.at[p],
                        device_id={"pipe": s, "dp": owner},
                    ).start()

    def drain():
        def drain_item(item, _):
            pltpu.make_async_copy(received.at[item], received.at[item], sent_sem.at[item]).wait()
            return 0

        lax.fori_loop(0, 2 * later, drain_item, 0)

        def drain_grads(s, _):
            pltpu.make_async_copy(half_send.at[s], half_send.at[s], half_send_sem.at[s]).wait()
            here = (place == s) & (replica // 2 == core)

            @pl.when(here)
            def _():
                pltpu.make_async_copy(chip_send.at[s, 0], chip_send.at[s, 0], chip_send_sem.at[s]).wait()

            @pl.when(jnp.logical_not(here))
            def _():
                pltpu.make_async_copy(chip_send.at[s], chip_send.at[s], chip_send_sem.at[s]).wait()

            return 0

        lax.fori_loop(0, SECTIONS, drain_grads, 0)

        @pl.when(in_window)
        def _():
            all_sent = tokens.at[:, pl.ds(0, (seq - 1) * HEAD)]
            pltpu.make_async_copy(all_sent, all_sent, in_send).wait()

    def own_sum():
        for p in range(2):
            at = half_rows(p)
            there = chip_recv.at[:, at]
            pltpu.make_async_copy(there, there, chip_recv_sem.at[p]).wait()
            part = chip_recv[0, at].astype(F32)
            for k in range(1, 2 * dp):
                part = part + chip_recv[k, at].astype(F32)
            own_send[at] = part.astype(BF16)
            for o in range(1, dp):
                pltpu.make_async_remote_copy(
                    src_ref=own_send.at[at],
                    dst_ref=own_recv.at[o - 1, at],
                    send_sem=own_send_sem.at[p],
                    recv_sem=own_recv_sem.at[p],
                    device_id={"dp": (replica + o) & (dp - 1)},
                ).start()
        grads_ref[0, 0, replica] = own_send[...]
        drain()
        for p in range(2):
            at = half_rows(p)
            there = own_recv.at[:, at]
            pltpu.make_async_copy(there, there, own_recv_sem.at[p]).wait()
            for o in range(1, dp):
                grads_ref[0, 0, (replica - o) & (dp - 1), at] = own_recv[o - 1, at]
        for p in range(2):
            there = own_recv.at[:, half_rows(p)]
            pltpu.make_async_copy(there, there, own_send_sem.at[p]).wait()

    def project(s, c, x):
        qkv = dot((x * gain_of(s)).astype(BF16), weights_in[s])
        q, k = qkv[:, :HEAD], qkv[:, HEAD : 2 * HEAD]
        raw[c, 0], raw[c, 1], raw[c, 2] = q, k, qkv[:, 2 * HEAD :]
        raw[c, 3] = dot((q * q).astype(BF16), mean)
        raw[c, 4] = dot((k * k).astype(BF16), mean)

    def arrived(c):
        for h in range(2):
            first = max(c * blocks, lead if h else 0)
            last = min((c + 1) * blocks, all_blocks if h else own_blocks + 1)

            @pl.when(half == h)
            def _():
                there = landing.at[pl.ds(first, last - first)]
                pltpu.make_async_copy(there, there, in_recv.at[c]).wait()

    def forward(i, _):
        s, c = i // chunks, i % chunks
        base = c * chunk
        whole = span_of(base, chunk)
        padded = span_of(base + SPAN, chunk)

        for k in range(chunks):
            @pl.when(i == k)
            def _():
                arrived(k)

        @pl.when(i < chunks)
        def _():
            new = jnp.concatenate([landing[c * blocks + b, :SPAN] for b in range(blocks)], axis=0)
            states[0, whole] = new
            project(0, c, new.astype(F32))
            left = lax.broadcasted_iota(jnp.int32, (1, HEAD), 1) < SPAN
            for g in range(groups):
                pair = []
                for b in (2 * g, min(2 * g + 1, blocks - 1)):
                    two = landing[c * blocks + b, SPAN:].astype(F32)
                    pair.append(two[:1] + two[1:2])
                current[g : g + 1] = jnp.where(left, pair[0], pair[1])

        @pl.when(i >= chunks)
        def _():
            current[...] = finish(i - chunks)

        wide = spread(lax.rsqrt(current[...] * (1.0 / width) + EPSILON))
        squared = wide * wide
        x = states[s, whole].astype(F32)
        rq = lax.rsqrt(squared * raw[c, 3] + EPSILON)
        rk = lax.rsqrt(squared * raw[c, 4] + EPSILON)
        qn = (raw[c, 0] * (wide * rq)).astype(BF16)
        kn = (raw[c, 1] * (wide * rk)).astype(BF16)
        v = (raw[c, 2] * wide).astype(BF16)
        near_k = jnp.concatenate([keys[s, span_of(base, SPAN)], kn], axis=0)
        near_v = jnp.concatenate([values[s, span_of(base, SPAN)], v], axis=0)
        scores = [dot_nt(cut(qn, b), cut(near_k, b, 2 * SPAN)) for b in range(blocks)]
        raised = [
            jnp.exp2(scores[b] * (LOG2E * HEAD**-0.5)).astype(BF16) * mask[c * blocks + b]
            for b in range(blocks)
        ]
        both = [
            dot(raised[b], jnp.concatenate([cut(near_v, b, 2 * SPAN), ones], axis=1))
            for b in range(blocks)
        ]
        inverse = [1.0 / both[b][:, HEAD:] for b in range(blocks)]
        o = jnp.concatenate([(both[b][:, :HEAD] * inverse[b]).astype(BF16) for b in range(blocks)], axis=0)
        branch = dot(o, weights[s, 3]).astype(BF16)
        new = (x + branch.astype(F32)).astype(BF16)
        wide_new = new.astype(F32)
        states[s + 1, whole] = new
        scale_x[s, whole] = wide
        queries[s, whole] = qn
        keys[s, padded] = kn
        values[s, padded] = v
        mixed[s, whole] = o

        @pl.when(s < SECTIONS - 1)
        def _():
            start(i, packed((wide_new * wide_new).astype(BF16)))
            project(s + 1, c, wide_new)

        scale_q[s, whole] = rq * HEAD**-0.5
        scale_k[s, whole] = rk * HEAD**-0.5
        for b in range(blocks):
            chances[s, c * blocks + b] = (raised[b].astype(F32) * inverse[b]).astype(BF16)
        normed[s, whole] = (x * wide * gain_of(s)).astype(BF16)
        return 0

    lax.fori_loop(0, SECTIONS * chunks, forward, 0)


    def backward(j, _):
        s, c = SECTIONS - 1 - j // chunks, chunks - 1 - j % chunks
        base = c * chunk
        whole = span_of(base, chunk)

        @pl.when(j < chunks)
        def _():
            cot[whole] = states[SECTIONS, whole] * valid[whole]

        @pl.when(j >= chunks)
        def _():
            along = spread(finish(later + j - chunks) * (1.0 / width))
            wide = scale_x[s + 1, whole]
            unit = states[s + 1, whole].astype(F32) * (wide * wide)
            cot[whole] = (base_cot[whole] - unit * along).astype(BF16)

        @pl.when(c == chunks - 1)
        def _():
            carry[...] = jnp.zeros_like(carry)

        g = cot[whole]
        o = mixed[s, whole]
        gm = dot(g, weights_back[s, 3 * HEAD :]).astype(BF16)
        delta = dot((gm.astype(F32) * o.astype(F32)).astype(BF16), ones)
        near = span_of(base, chunk + SPAN)
        near_k, near_v = keys[s, near], values[s, near]
        qn = queries[s, whole]
        share = [chances[s, c * blocks + b] for b in range(blocks)]
        unit_v = [dot_tn(share[b], cut(gm, b)) for b in range(blocks)]
        late_v = [unit_v[b][:SPAN] for b in range(1, blocks)] + [carry[1]]
        carry[1] = unit_v[0][:SPAN]
        all_v = jnp.concatenate([unit_v[b][SPAN:] + late_v[b] for b in range(blocks)], axis=0)
        dv = all_v.astype(BF16)
        xn = normed[s, whole]

        grad_share = [dot_nt(cut(gm, b), cut(near_v, b, 2 * SPAN)) for b in range(blocks)]
        grad_score = [
            (share[b].astype(F32) * (grad_share[b] - cut(delta, b))).astype(BF16) for b in range(blocks)
        ]
        unit_q = [dot(grad_score[b], cut(near_k, b, 2 * SPAN)) for b in range(blocks)]
        unit_k = [dot_tn(grad_score[b], cut(qn, b)) for b in range(blocks)]
        late_k = [unit_k[b][:SPAN] for b in range(1, blocks)] + [carry[0]]
        all_k = jnp.concatenate([unit_k[b][SPAN:] + late_k[b] for b in range(blocks)], axis=0)
        carry[0] = unit_k[0][:SPAN]
        all_q = jnp.concatenate(unit_q, axis=0)
        wide_q = qn.astype(F32)
        wide_k = near_k[SPAN:].astype(F32)
        terms_q = all_q * wide_q
        terms_k = all_k * wide_k
        sq, sk = scale_q[s, whole], scale_k[s, whole]

        @pl.when(s > 0)
        def _():
            small = (EPSILON * HEAD**0.5) * (sq * sq * terms_q + sk * sk * terms_k)
            start(later + j, packed((all_v * near_v[SPAN:].astype(F32) + small).astype(BF16)))

        along_q = dot(terms_q.astype(BF16), mean)
        along_k = dot(terms_k.astype(BF16), mean)
        dq = (sq * (all_q - wide_q * along_q)).astype(BF16)
        dk = (sk * (all_k - wide_k * along_k)).astype(BF16)
        joined = jnp.concatenate([dq, dk, dv], axis=1)

        @pl.when(s > 0)
        def _():
            grad = dot(joined, weights_back[s, : 3 * HEAD]).astype(BF16)
            base_cot[whole] = g.astype(F32) + scale_x[s, whole] * (grad.astype(F32) * gain_of(s))

        both = dot_tn(xn, joined[:, : 2 * HEAD])
        sums[s, 0] += both[:, :HEAD]
        sums[s, 1] += both[:, HEAD:]

        @pl.when(s >= 0)
        def _():
            sums[s, 2] += dot_tn(normed[s, whole], all_v.astype(BF16))
            sums[s, 3] += dot_tn(mixed[s, whole], cot[whole])

        @pl.when(c == 0)
        def _():
            start_halves(s)

        @pl.when((c == 0) & (s > 0))
        def _():
            start_chips(s)

        return 0

    lax.fori_loop(0, SECTIONS * chunks, backward, 0)

    start_chips(0)
    own_sum()


def local(inputs, weights, gains, doc_lengths):
    seq, pipe, dp = lax.axis_size("seq"), lax.axis_size("pipe"), lax.axis_size("dp")
    total = inputs.shape[2] * seq
    width = gains.shape[1]
    rows = total // 2 + 2 * SPAN
    chunks = 2
    chunk = rows // chunks
    across = 4 if seq > 4 else 2
    down = seq // across
    items = 2 * (SECTIONS - 1) * chunks
    groups = -(-chunk // GROUP)
    cfg = dict(
        total=total,
        seq=seq,
        pipe=pipe,
        dp=dp,
        width=width,
        across=across,
        rows=rows,
        chunk=chunk,
        chunks=chunks,
    )
    scratch = [
        pltpu.VMEM((SECTIONS, 4, HEAD, HEAD), BF16),
        pltpu.VMEM((SECTIONS, HEAD), F32),
        pltpu.VMEM(doc_lengths.shape[1:], jnp.int32),
        pltpu.VMEM((SECTIONS, HEAD, 3 * HEAD), BF16),
        pltpu.VMEM((SECTIONS, 4 * HEAD, HEAD), BF16),
        pltpu.VMEM((SECTIONS + 1, rows, HEAD), BF16),
        pltpu.VMEM((SECTIONS, rows, HEAD), BF16),
        pltpu.VMEM((SECTIONS, rows, HEAD), BF16),
        pltpu.VMEM((SECTIONS, SPAN + rows, HEAD), BF16),
        pltpu.VMEM((SECTIONS, SPAN + rows, HEAD), BF16),
        pltpu.VMEM((SECTIONS, rows, HEAD), BF16),
        pltpu.VMEM((SECTIONS, rows // SPAN, SPAN, 2 * SPAN), BF16),
        pltpu.VMEM((SECTIONS, rows, HEAD), F32),
        pltpu.VMEM((SECTIONS, rows, HEAD), F32),
        pltpu.VMEM((SECTIONS, rows, HEAD), F32),
        pltpu.VMEM((rows // SPAN, SPAN, 2 * SPAN), BF16),
        pltpu.VMEM((rows, HEAD), BF16),
        pltpu.VMEM((rows, HEAD), BF16),
        pltpu.VMEM((rows, HEAD), F32),
        pltpu.VMEM((2, SPAN, HEAD), F32),
        pltpu.VMEM((SECTIONS, 4, HEAD, HEAD), F32),
        pltpu.VMEM((SECTIONS, 8, HEAD), F32),
        pltpu.VMEM((SPAN + EXTRA, width), BF16),
        pltpu.VMEM((rows // SPAN, SPAN + EXTRA, HEAD), BF16),
        pltpu.VMEM((chunks, 5, chunk, HEAD), F32),
        pltpu.VMEM((8, HEAD), F32),
        pltpu.VMEM((items, groups, HEAD), F32),
        pltpu.VMEM((items, seq - 1, groups, HEAD), F32),
        pltpu.VMEM((SECTIONS, 2, HEAD, HEAD), BF16),
        pltpu.VMEM((SECTIONS, 2, HEAD, HEAD), BF16),
        pltpu.VMEM((SECTIONS, 2, HEAD, HEAD), BF16),
        pltpu.VMEM((2 * dp, HEAD, HEAD), BF16),
        pltpu.VMEM((HEAD, HEAD), BF16),
        pltpu.VMEM((dp - 1, HEAD, HEAD), BF16),
        pltpu.SemaphoreType.DMA((4,)),
        pltpu.SemaphoreType.DMA,
        pltpu.SemaphoreType.DMA((chunks,)),
        pltpu.SemaphoreType.DMA((items,)),
        pltpu.SemaphoreType.DMA((items,)),
        pltpu.SemaphoreType.DMA((SECTIONS,)),
        pltpu.SemaphoreType.DMA((SECTIONS,)),
        pltpu.SemaphoreType.DMA((SECTIONS,)),
        pltpu.SemaphoreType.DMA((2,)),
        pltpu.SemaphoreType.DMA((2,)),
        pltpu.SemaphoreType.DMA((2,)),
    ]
    hbm = pl.BlockSpec(memory_space=pltpu.HBM)
    return pl.pallas_call(
        functools.partial(kernel, cfg),
        out_shape=jax.ShapeDtypeStruct((1, 1, 4, HEAD, HEAD), BF16),
        in_specs=[hbm, hbm, hbm, hbm],
        out_specs=pl.BlockSpec(memory_space=pltpu.VMEM),
        scratch_shapes=scratch,
        compiler_params=pltpu.CompilerParams(
            collective_id=0, has_side_effects=True, vmem_limit_bytes=60 * 1024 * 1024
        ),
    )(inputs, weights, gains, doc_lengths).astype(F32)


def solution(mesh):
    placed = (
        P("dp", None, "seq", None),
        P(None, "seq", None, None, None),
        P(),
        P("dp", None, None),
    )
    return jax.shard_map(
        local,
        mesh=mesh,
        in_specs=placed,
        out_specs=P("pipe", "seq", None, None, None),
        check_vma=False,
    )
```
